128 devices in a mesh: dom: 32 (over z, x, core), sub: 4 (over y).
Axes of the slice: x: 4, y: 4, z: 4, core: 2. Of those that a mesh axis runs over, the one named last changes fastest.
Arguments:
- start_block: bfloat16 [64, 524288], P(None, ('dom', 'sub')), may hold values from -6 to 6
- tiles_in: bfloat16 [4096, 12, 128, 128], P(('dom', 'sub')), may hold values from -86 to 86, as said below
- tiles_out: bfloat16 [4096, 4, 128, 128], P(('dom', 'sub')), may hold values from -86 to 86, as said below
- in_cols: int32 [4096, 12], P(('dom', 'sub')), may hold values from 0 to 127
- out_cols: int32 [4096, 4], P(('dom', 'sub')), may hold values from 0 to 127
- export_list: int32 [32, 4, 4], P('dom', 'sub'), may hold values from 0 to 127
- recv_list: int32 [32, 4, 32, 4], P('dom', 'sub'), may hold values from 0 to 3
Outputs:
- basis: float32 [64, 524288], P(None, ('dom', 'sub'))
- projected: float32 [64, 64], replicated
The draws below stay inside these ranges and needn't reach their ends.
Inputs may be any that keep to these rules, and one draw needn't show every extreme that they name: `tiles_in`: tile weights; row magnitudes differ over the graph. `tiles_out`: laid out as tiles_in, with the same row magnitudes.
All inputs are finite; a program needn't handle non-finite values.
Results may differ from the reference program's by a relative error of at most 0.0057.
Values may be sent and summed in bfloat16 or wider, within the bound.
A program may use at most 128 MiB of HBM per device.

```python
import math
import jax
import jax.numpy as jnp
from jax import lax

K = 64
TILE = 128
BLK_DEV = 32
TP_IN = 12
TP_OUT = 4
CAP = 4
EXPORTS = 4
PART_BLOCKS = 128
ROW_BLOCKS = 4096
ROWS = 524288
N_DOM = 32
N_SUB = 4


def row_scales(key):
    rough = jax.random.uniform(key, (ROW_BLOCKS, 1, 1, TILE), jnp.float32, -0.35, 0.35)
    position = (jnp.arange(ROW_BLOCKS)[:, None] * TILE + jnp.arange(TILE)[None, :]).astype(jnp.float32) / ROWS
    return jnp.exp(math.log(10.0) * position.reshape(ROW_BLOCKS, 1, 1, TILE) + rough)


def tile_values(key, count):
    shape = (ROW_BLOCKS, count, TILE, TILE)
    values = jnp.clip(jax.random.normal(key, shape, jnp.float32), -6.0, 6.0)
    return values


def draw_tiles_in(key, part):
    scales = row_scales(key)
    key = jax.random.fold_in(key, 11)
    return (tile_values(key, TP_IN) * scales).astype(jnp.bfloat16)


def draw_tiles_out(key, part):
    scales = row_scales(key)
    key = jax.random.fold_in(key, 23)
    return (tile_values(key, TP_OUT) * scales).astype(jnp.bfloat16)


def place_ends(drawn, own_key, least, largest):
    longest = drawn.shape.index(max(drawn.shape))
    spots = []
    for shift in (0, 1):
        where = [jax.random.randint(jax.random.fold_in(own_key, axis), (), 0, length) for axis, length in enumerate(drawn.shape)]
        where[longest] = (where[longest] + shift) % drawn.shape[longest]
        spots.append(tuple(where))
    return drawn.at[spots[0]].set(least).at[spots[1]].set(largest)


def block_scale(rng, shape, cuts, least, largest):
    level = 1.0
    for dim, blocks in cuts:
        heights = jax.random.uniform(jax.random.fold_in(jax.random.fold_in(rng, 6), dim), (blocks,), jnp.float32, least / len(cuts), largest / len(cuts))
        level = level * jnp.repeat(jnp.exp(heights), shape[dim] // blocks).reshape((-1,) + (1,) * (len(shape) - 1 - dim))
    return level


def noise(rng, shape, width, bound, shards=(), held_as=jnp.bfloat16):
    drawn = jax.random.normal(rng, shape, jnp.float32) * width
    if len(shards) > 0:
        drawn = block_scale(rng, shape, shards, -0.22, 0.18) * drawn
    return jnp.clip(drawn, min=-bound, max=bound).astype(held_as)


def setup_inputs(seed: int = 0) -> dict:
    key_list = jax.random.split(jax.random.key(seed), 8)
    start_block = noise(key_list[0], (K, ROWS), 1.0, 6.0, ((1, 128),))
    tiles_in = draw_tiles_in(jax.random.fold_in(key_list[7], 71), 0)
    tiles_out = draw_tiles_out(jax.random.fold_in(key_list[7], 71), 0)
    in_cols = place_ends(jax.random.randint(key_list[3], (ROW_BLOCKS, TP_IN), 0, PART_BLOCKS), jax.random.fold_in(key_list[3], 1), 0, PART_BLOCKS - 1).astype(jnp.int32)
    out_cols = place_ends(jax.random.randint(key_list[4], (ROW_BLOCKS, TP_OUT), 0, N_DOM * CAP), jax.random.fold_in(key_list[4], 1), 0, (N_DOM * CAP) - 1).astype(jnp.int32)
    export_list = place_ends(jax.random.randint(key_list[5], (N_DOM, N_SUB, EXPORTS), 0, PART_BLOCKS), jax.random.fold_in(key_list[5], 1), 0, PART_BLOCKS - 1).astype(jnp.int32)
    recv_list = place_ends(jax.random.randint(key_list[6], (N_DOM, N_SUB, N_DOM, CAP), 0, EXPORTS), jax.random.fold_in(key_list[6], 1), 0, EXPORTS - 1).astype(jnp.int32)
    return {"start_block": start_block, "tiles_in": tiles_in, "tiles_out": tiles_out, "in_cols": in_cols, "out_cols": out_cols, "export_list": export_list, "recv_list": recv_list}


def column_blocks(in_cols, out_cols, export_list, recv_list):
    device = jnp.arange(ROW_BLOCKS, dtype=jnp.int32) // BLK_DEV
    owner = (device // N_SUB)[:, None]
    within = (device % N_SUB)[:, None]
    in_global = owner * PART_BLOCKS + in_cols
    source = out_cols // CAP
    column = out_cols % CAP
    position = recv_list[owner, within, source, column]
    block = export_list[source, within, position]
    out_global = source * PART_BLOCKS + block
    return (in_global.astype(jnp.int32), out_global.astype(jnp.int32))

def reference(start_block, tiles_in, tiles_out, in_cols, out_cols, export_list, recv_list):
    in_global, out_global = column_blocks(in_cols, out_cols, export_list, recv_list)
    count = (TP_IN + TP_OUT) * TILE
    magnitude = (lax.optimization_barrier(jnp.sum(jnp.abs(tiles_in), axis=(1, 2), dtype=jnp.float32)) + lax.optimization_barrier(jnp.sum(jnp.abs(tiles_out), axis=(1, 2), dtype=jnp.float32))) / count + 1e-06
    inverse_root = (1.0 / jnp.sqrt(magnitude)).reshape(ROWS)
    spectral = 1.0 / (1.25 * math.sqrt(count))
    devices = N_DOM * N_SUB
    grouped_in = tiles_in.reshape(devices, BLK_DEV, TP_IN, TILE, TILE)
    grouped_out = tiles_out.reshape(devices, BLK_DEV, TP_OUT, TILE, TILE)
    index_in = in_global.reshape(devices, BLK_DEV, TP_IN)
    index_out = out_global.reshape(devices, BLK_DEV, TP_OUT)

    def operate(vectors):
        scaled = (vectors * inverse_root[None, :]).astype(jnp.bfloat16).reshape(K, ROW_BLOCKS, TILE)

        def one_device(pieces):
            near_tiles, far_tiles, near_index, far_index = pieces
            inner = jnp.einsum('kbpc,bpcr->kbr', scaled[:, near_index].astype(jnp.float32), near_tiles.astype(jnp.float32))
            outer = jnp.einsum('kbpc,bpcr->kbr', scaled[:, far_index].astype(jnp.float32), far_tiles.astype(jnp.float32))
            return inner + outer
        summed = lax.map(one_device, (grouped_in, grouped_out, index_in, index_out))
        summed = jnp.transpose(summed, (1, 0, 2, 3)).reshape(K, ROWS)
        return summed * (spectral * inverse_root)[None, :]
    first = start_block.astype(jnp.float32)
    second = operate(first)
    third = 2.0 * operate(second) - first
    filtered = 2.0 * operate(third) - second
    image = operate(filtered)
    gram = jnp.dot(filtered, filtered.T, precision=lax.Precision.HIGHEST) / ROWS
    rayleigh = jnp.dot(filtered, image.T, precision=lax.Precision.HIGHEST) / ROWS
    lower = jnp.linalg.cholesky(gram)
    basis = jax.scipy.linalg.solve_triangular(lower, filtered, lower=True)
    halfway = jax.scipy.linalg.solve_triangular(lower, rayleigh, lower=True)
    projected = jax.scipy.linalg.solve_triangular(lower, halfway.T, lower=True).T
    return (basis, projected)
```

```python
import functools
import math

import jax
import jax.numpy as jnp
from jax import lax
from jax.experimental import pallas as pl
from jax.experimental.pallas import tpu as pltpu
from jax.sharding import PartitionSpec as P

MESH = pl.DeviceIdType.MESH
HIGHEST = lax.Precision.HIGHEST
F32 = jnp.float32
BF16 = jnp.bfloat16
OPS = 4
NC = 4


def nt(a, b):
    return lax.dot_general(
        a, b, (((1,), (1,)), ((), ())), precision=HIGHEST, preferred_element_type=F32
    )


def kernel(
    rows_total, spectral, count,
    start_ref, tin_hbm, tout_hbm, ic, oc, exp_ref, recv_ref,
    basis_ref, proj_ref,
    tin, tout, *scratch,
):
    parts = [scratch[NC * p : NC * p + NC] for p in range(2)]
    scratch = scratch[2 * NC :]
    outs = [scratch[NC * p : NC * p + NC] for p in range(2)]
    (vec, acc, dinv, rowf, oidx, mat, gram_bufs, ray_bufs,
     load_sem, y_send, y_recv, xz_send, xz_recv, core_send, core_recv,
     ar_send, ar_recv) = scratch[2 * NC :]
    width = start_ref.shape[0]
    kc = width // NC
    nb, tp_in = tin.shape[:2]
    tp_out = tout.shape[1]
    tile = tin.shape[2]
    half = nb // 2
    offered = exp_ref.shape[0]

    dom = lax.axis_index("dom")
    s = lax.axis_index("sub")
    z, x, core = dom // 8, (dom // 2) % 4, dom % 2

    def dev(dz, dx, dy, dc):
        zz, xx, cc = (z + dz) % 4, (x + dx) % 4, (core + dc) % 2
        return (zz * 8 + xx * 2 + cc, (s + dy) % 4)

    plane = [(dz, dx) for dz in range(4) for dx in range(4) if (dz, dx) != (0, 0)]
    right, left, partner = dev(0, 0, 1, 0), dev(0, 0, 3, 0), dev(0, 0, 0, 1)

    barrier = pltpu.get_barrier_semaphore()
    friends = [dev(dz, dx, 0, 0) for dz, dx in plane]
    friends += [dev(0, 0, dy, 0) for dy in (1, 2, 3)] + [partner]
    for f in friends:
        pl.semaphore_signal(barrier, inc=1, device_id=f, device_id_type=MESH)

    pieces = load_sem.shape[0]
    step = nb // pieces
    loads = []
    for i in range(pieces):
        rows = pl.ds(i * step, step)
        a = pltpu.make_async_copy(tin_hbm.at[rows], tin.at[rows], load_sem.at[i, 0])
        b = pltpu.make_async_copy(tout_hbm.at[rows], tout.at[rows], load_sem.at[i, 1])
        a.start()
        b.start()
        loads.append((a, b))

    def slot_of(i, carry):
        b, t = i // tp_out, i % tp_out
        v = oc[b, t]
        g = v // offered
        oidx[b, t] = (g % 2) * (16 * offered) + (g // 2) * offered + recv_ref[v]
        return carry

    lax.fori_loop(0, nb * tp_out, slot_of, 0)
    for b in range(nb):
        vec[0, b] = start_ref[:, b * tile : (b + 1) * tile].astype(F32)

    def total(ref, b, n):
        a = jnp.abs(ref[b].reshape(n * tile, tile)).astype(F32)
        return jnp.sum(a.reshape(n * tile // 8, 8, tile), axis=0)

    for i in range(pieces):
        for cp in loads[i]:
            cp.wait()

        def degree(b, carry):
            mag = jnp.sum(total(tin, b, tp_in) + total(tout, b, tp_out), axis=0, keepdims=True)
            inv = 1.0 / jnp.sqrt(mag / count + 1e-06)
            dinv[b] = jnp.broadcast_to(inv, (8, tile))
            rowf[b] = jnp.broadcast_to(spectral * inv, (8, tile))
            return carry

        lax.fori_loop(i * step, (i + 1) * step, degree, 0, unroll=2)

    pl.semaphore_wait(barrier, len(friends))

    own = s * nb
    base = core * (16 * offered) + (z * 4 + x) * offered

    def y_copies(j):
        part = parts[(j // NC) % 2][j % NC]

        def cp(k, first, to):
            block = part.at[pl.ds(first, half)]
            return pltpu.make_async_remote_copy(
                src_ref=block, dst_ref=block, send_sem=y_send.at[j, k],
                recv_sem=y_recv.at[j, k], device_id=to, device_id_type=MESH,
            )

        lo = ((s + 3) % 4) * nb
        hi = ((s + 1) % 4) * nb
        sends = [cp(0, own, right), cp(1, own + half, left), cp(2, own + half, right), cp(3, own, left)]
        forwards = [cp(4, lo, right), cp(5, hi + half, left)]
        return sends, forwards

    def send_own(j):
        for cp in y_copies(j)[0]:
            cp.start()

    def forward(j):
        sends, forwards = y_copies(j)
        for k in range(2):
            sends[k].wait_recv()
            forwards[k].start()

    def xz_copies(j):
        out = outs[(j // NC) % 2][j % NC]
        block = out.at[pl.ds(base, offered)]
        return [
            pltpu.make_async_remote_copy(
                src_ref=block, dst_ref=block, send_sem=xz_send.at[j], recv_sem=xz_recv.at[j],
                device_id=dev(dz, dx, 0, 0), device_id_type=MESH,
            )
            for dz, dx in plane
        ]

    def wait_bytes(out, sem):
        view = out.at[pl.ds(0, len(plane) * offered)]
        pltpu.make_async_copy(view, view, sem).wait()

    def export(j):
        sends, forwards = y_copies(j)
        sends[2].wait_recv()
        sends[3].wait_recv()
        for cp in forwards:
            cp.wait_recv()
        for cp in sends:
            cp.wait_send()
        part = parts[(j // NC) % 2][j % NC]
        out = outs[(j // NC) % 2][j % NC]
        for e in range(offered):
            out[base + e] = part[exp_ref[e]]
        for cp in xz_copies(j):
            cp.start()

    def core_copy(j):
        block = outs[(j // NC) % 2][j % NC].at[pl.ds(core * (16 * offered), 16 * offered)]
        return pltpu.make_async_remote_copy(
            src_ref=block, dst_ref=block, send_sem=core_send.at[j], recv_sem=core_recv.at[j],
            device_id=partner, device_id_type=MESH,
        )

    def share(j):
        out = outs[(j // NC) % 2][j % NC]
        wait_bytes(out, xz_recv.at[j])
        core_copy(j).start()
        wait_bytes(out, xz_send.at[j])
        for cp in y_copies(j)[1]:
            cp.wait_send()

    def inner(j, first, last):
        part, c = parts[(j // NC) % 2][j % NC], j % NC

        def one(b, carry):
            v = jnp.concatenate([part[ic[b, t]] for t in range(tp_in)], axis=1)
            acc[c, b] = jnp.dot(v, tin[b].reshape(tp_in * tile, tile), preferred_element_type=F32)
            return carry

        lax.fori_loop(first, last, one, 0, unroll=4)

    def scale(part, c, b, new):
        part[own + b] = (new * dinv[b, :1, :]).astype(BF16)

    def outer(j):
        n, c = j // NC, j % NC
        core_copy(j).wait_recv()
        core_copy(j).wait_send()
        out = outs[n % 2][c]
        rows = pl.ds(c * kc, kc)
        p = (n + 1) % 2

        def one(b, carry):
            v = jnp.concatenate([out[oidx[b, t]] for t in range(tp_out)], axis=1)
            o = acc[c, b] + jnp.dot(v, tout[b].reshape(tp_out * tile, tile), preferred_element_type=F32)
            new = o * rowf[b, :1, :]
            if n in (1, 2):
                new = 2.0 * new - vec[p, b, rows, :]
            vec[p, b, rows, :] = new
            if n + 1 < OPS:
                scale(parts[p][c], c, b, new)
            return carry

        lax.fori_loop(0, nb, one, 0, unroll=4)

    axes = [
        (core, [dev(0, 0, 0, 1)]),
        (s, [dev(0, 0, d, 0) for d in (1, 2, 3)]),
        (x, [dev(0, d, 0, 0) for d in (1, 2, 3)]),
        (z, [dev(d, 0, 0, 0) for d in (1, 2, 3)]),
    ]

    def sum_copies(use, a):
        bufs = (gram_bufs, ray_bufs)[use]
        place, peers = axes[a]
        block = bufs.at[a, place]
        return [
            pltpu.make_async_remote_copy(
                src_ref=block, dst_ref=block, send_sem=ar_send.at[use, a], recv_sem=ar_recv.at[use, a],
                device_id=to, device_id_type=MESH,
            )
            for to in peers
        ]

    def sum_start(use, a, value):
        bufs = (gram_bufs, ray_bufs)[use]
        bufs[a, axes[a][0]] = value
        for cp in sum_copies(use, a):
            cp.start()

    def sum_end(use, a):
        bufs = (gram_bufs, ray_bufs)[use]
        n = len(axes[a][1])
        view = bufs.at[a, pl.ds(0, n)]
        pltpu.make_async_copy(view, view, ar_recv.at[use, a]).wait()
        pltpu.make_async_copy(view, view, ar_send.at[use, a]).wait()
        value = bufs[a, 0] + bufs[a, 1]
        for k in range(2, n + 1):
            value = value + bufs[a, k]
        return value

    fslot = OPS % 2 ^ 1
    group = 4

    def wide(slot, i, rows):
        return jnp.concatenate([vec[slot, i * group + k, rows, :] for k in range(group)], axis=1)

    def product(slot):
        def one(i, carry):
            return carry + nt(wide(slot, i, slice(None)), wide(fslot, i, slice(None)))

        zero = jnp.zeros((width, width), F32)
        got = lax.fori_loop(0, nb // group, one, zero)
        return jnp.concatenate([got, zero], axis=1)

    lane = lax.broadcasted_iota(jnp.int32, (1, 2 * width), 1)
    line = lax.broadcasted_iota(jnp.int32, (width, 1), 0)

    def eliminate(first, last):
        def one(k, carry):
            m = mat[...]
            row = mat[pl.ds(k, 1), :]
            inv = 1.0 / jnp.sqrt(jnp.sum(jnp.where(lane == k, row, 0.0), axis=1, keepdims=True))
            row = row * inv
            col = jnp.sum(jnp.where(lane == k, m, 0.0), axis=1, keepdims=True) * inv
            mat[...] = jnp.where(line > k, m - col * row, jnp.where(line == k, row, m))
            return carry

        lax.fori_loop(first, last, one, 0)

    def start_elimination(gram):
        eye = jnp.where(lane - width == line, 1.0, 0.0)
        mat[...] = jnp.where(lane < width, gram / rows_total, eye)

    for c in range(NC):
        def one(b, carry, c=c):
            scale(parts[0][c], c, b, vec[0, b, c * kc : (c + 1) * kc, :])
            return carry

        lax.fori_loop(0, nb, one, 0, unroll=4)
        send_own(c)

    stages = OPS * NC

    def has(j):
        return 0 <= j < stages

    for i in range(1, stages + NC):
        if i >= NC and has(i - 4):
            outer(i - 4)
        if i >= NC and has(i):
            send_own(i)
        if has(i - 1):
            forward(i - 1)
        if i == stages:
            sum_start(0, 0, product(fslot))
        if has(i - 2):
            export(i - 2)
            inner(i - 2, 0, nb // 2)
        if i == stages:
            sum_start(0, 1, sum_end(0, 0))
        if i == stages + 1:
            sum_start(0, 3, sum_end(0, 2))
        if has(i - 3):
            share(i - 3)
        if has(i - 2):
            inner(i - 2, nb // 2, nb)
        if i == stages:
            sum_start(0, 2, sum_end(0, 1))
        if i == stages + 1:
            start_elimination(sum_end(0, 3))
        if i == stages + 2:
            eliminate(0, width)

    sum_start(1, 0, product(1 - fslot))
    linv = mat[...][:, width:]
    for a in range(4):
        for i in range(a * 2, a * 2 + 2):
            got = jnp.dot(linv, wide(fslot, i, slice(None)), precision=HIGHEST, preferred_element_type=F32)
            basis_ref[:, i * group * tile : (i + 1) * group * tile] = got
        value = sum_end(1, a)
        if a < 3:
            sum_start(1, a + 1, value)
    rayleigh_t = value[:, :width] / rows_total
    proj_ref[...] = nt(nt(linv, rayleigh_t), linv)


def body(start_block, tiles_in, tiles_out, in_cols, out_cols, export_list, recv_list):
    width, local_rows = start_block.shape
    nb, tp_in, tile, _ = tiles_in.shape
    tp_out = tiles_out.shape[1]
    count = (tp_in + tp_out) * tile
    devices = lax.axis_size("dom") * lax.axis_size("sub")
    kc = width // NC
    stages = OPS * NC
    blocks = nb * 4
    slots = recv_list.size
    smem = pl.BlockSpec(memory_space=pltpu.SMEM)
    hbm = pl.BlockSpec(memory_space=pl.ANY)
    vmem = pl.BlockSpec(memory_space=pltpu.VMEM)
    dma = pltpu.SemaphoreType.DMA
    return pl.pallas_call(
        functools.partial(
            kernel, local_rows * devices, 1.0 / (1.25 * math.sqrt(count)), count
        ),
        out_shape=(
            jax.ShapeDtypeStruct((width, local_rows), F32),
            jax.ShapeDtypeStruct((width, width), F32),
        ),
        in_specs=[vmem, hbm, hbm, smem, smem, smem, smem],
        out_specs=(vmem, vmem),
        scratch_shapes=[
            pltpu.VMEM(tiles_in.shape, BF16),
            pltpu.VMEM(tiles_out.shape, BF16),
            *[pltpu.VMEM((blocks, kc, tile), BF16) for _ in range(2 * NC)],
            *[pltpu.VMEM((slots, kc, tile), BF16) for _ in range(2 * NC)],
            pltpu.VMEM((2, nb, width, tile), F32),
            pltpu.VMEM((NC, nb, kc, tile), F32),
            pltpu.VMEM((nb, 8, tile), F32),
            pltpu.VMEM((nb, 8, tile), F32),
            pltpu.SMEM((nb, tp_out), jnp.int32),
            pltpu.VMEM((width, 2 * width), F32),
            pltpu.VMEM((4, 4, width, 2 * width), F32),
            pltpu.VMEM((4, 4, width, 2 * width), F32),
            dma((8, 2)),
            dma((stages, 6)),
            dma((stages, 6)),
            dma((stages,)),
            dma((stages,)),
            dma((stages,)),
            dma((stages,)),
            dma((2, 4)),
            dma((2, 4)),
        ],
        compiler_params=pltpu.CompilerParams(
            collective_id=0, has_side_effects=True, vmem_limit_bytes=48 << 20
        ),
        name="filtered_step",
    )(
        start_block, tiles_in, tiles_out, in_cols, out_cols,
        export_list.reshape(-1), recv_list.reshape(-1),
    )


def solution(mesh):
    return jax.shard_map(
        body,
        mesh=mesh,
        in_specs=(
            P(None, ("dom", "sub")),
            P(("dom", "sub"), None, None, None),
            P(("dom", "sub"), None, None, None),
            P(("dom", "sub"), None),
            P(("dom", "sub"), None),
            P("dom", "sub", None),
            P("dom", "sub", None, None),
        ),
        out_specs=(P(None, ("dom", "sub")), P()),
        check_vma=False,
    )
```

```python
import functools
import math

import jax
import jax.numpy as jnp
from jax import lax
from jax.experimental import pallas as pl
from jax.experimental.pallas import tpu as pltpu
from jax.sharding import PartitionSpec as P

MESH = pl.DeviceIdType.MESH
HIGHEST = lax.Precision.HIGHEST
F32 = jnp.float32
BF16 = jnp.bfloat16
OPS = 4
NC = 4


def nt(a, b):
    return lax.dot_general(
        a, b, (((1,), (1,)), ((), ())), precision=HIGHEST, preferred_element_type=F32
    )


def kernel(
    rows_total, spectral, count,
    start_hbm, tin_hbm, tout_hbm, ic_hbm, oc_hbm, exp_hbm, recv_hbm,
    basis_ref, proj_ref,
    start_ref, tin, tout, *scratch,
):
    raws = scratch[:NC]
    scratch = scratch[NC:]
    parts = [scratch[NC * p : NC * p + NC] for p in range(2)]
    scratch = scratch[2 * NC :]
    outs = [scratch[NC * p : NC * p + NC] for p in range(2)]
    (vec, acc, dinv, rowf, dall, ic, oc, exp_ref, recv_ref, oidx, mat, ray, near, far, basis_vmem,
     table_sem, start_sem, load_sem, d_send, d_recv, y_send, y_recv, xz_send, xz_recv, core_send, core_recv,
     sum_send, sum_recv, basis_sem) = scratch[2 * NC :]
    width = start_ref.shape[0]
    kc = width // NC
    nb, tp_in = tin.shape[:2]
    tp_out = tout.shape[1]
    tile = tin.shape[2]
    half = nb // 2
    offered = exp_hbm.shape[0]

    dom = lax.axis_index("dom")
    s = lax.axis_index("sub")
    z, x, core = dom // 8, (dom // 2) % 4, dom % 2

    def dev(dz, dx, dy, dc):
        zz, xx, cc = (z + dz) % 4, (x + dx) % 4, (core + dc) % 2
        return (zz * 8 + xx * 2 + cc, (s + dy) % 4)

    plane = [(dz, dx) for dz in range(4) for dx in range(4) if (dz, dx) != (0, 0)]
    right, left, partner = dev(0, 0, 1, 0), dev(0, 0, 3, 0), dev(0, 0, 0, 1)

    barrier = pltpu.get_barrier_semaphore()
    friends = [dev(dz, dx, 0, 0) for dz, dx in plane]
    friends += [dev(0, 0, dy, dc) for dy in range(4) for dc in range(2) if (dy, dc) != (0, 0)]
    for f in friends:
        pl.semaphore_signal(barrier, inc=1, device_id=f, device_id_type=MESH)

    start_copy = pltpu.make_async_copy(start_hbm, start_ref, start_sem)
    start_copy.start()
    pieces = load_sem.shape[0]
    step = nb // pieces
    loads = []
    for i in range(pieces):
        rows = pl.ds(i * step, step)
        a = pltpu.make_async_copy(tin_hbm.at[rows], tin.at[rows], load_sem.at[i, 0])
        b = pltpu.make_async_copy(tout_hbm.at[rows], tout.at[rows], load_sem.at[i, 1])
        a.start()
        b.start()
        loads.append((a, b))

    own = s * nb
    table_copies = [
        pltpu.make_async_copy(a, b, table_sem.at[i])
        for i, (a, b) in enumerate(((ic_hbm, ic), (oc_hbm, oc), (exp_hbm, exp_ref), (recv_hbm, recv_ref)))
    ]
    for cp in table_copies:
        cp.start()

    def slot_of(i, carry):
        b, t = i // tp_out, i % tp_out
        v = oc[t, b]
        g, e = v // offered, v % offered
        oidx[t, b] = (g % 2) * (16 * offered) + (g // 2) * offered + recv_ref[e, g]
        return carry

    def total(ref, b, n):
        a = jnp.abs(ref[b].reshape(n * tile, tile)).astype(F32)
        return jnp.sum(a.reshape(n * tile // 8, 8, tile), axis=0)

    def degrees(first, last):
        for i in range(first, last):
            for cp in loads[i]:
                cp.wait()

            def degree(b, carry):
                mag = jnp.sum(total(tin, b, tp_in) + total(tout, b, tp_out), axis=0, keepdims=True)
                inv = 1.0 / jnp.sqrt(mag / count + 1e-06)
                dall[pl.ds(own + b, 1), :] = inv
                dinv[b] = jnp.broadcast_to(inv, (8, tile))
                rowf[b] = jnp.broadcast_to(spectral * inv, (8, tile))
                return carry

            lax.fori_loop(i * step, (i + 1) * step, degree, 0, unroll=True)

    def degree_copies():
        block = dall.at[pl.ds(own, nb)]
        return [
            pltpu.make_async_remote_copy(
                src_ref=block, dst_ref=block, send_sem=d_send, recv_sem=d_recv,
                device_id=dev(0, 0, d, 0), device_id_type=MESH,
            )
            for d in (1, 2, 3)
        ]

    def degrees_end():
        view = dall.at[pl.ds(0, 3 * nb)]
        pltpu.make_async_copy(view, view, d_recv).wait()
        pltpu.make_async_copy(view, view, d_send).wait()

    base = core * (16 * offered) + (z * 4 + x) * offered

    def y_copies(j):
        part = raws[j] if j < NC else parts[(j // NC) % 2][j % NC]

        def cp(k, first, to):
            block = part.at[pl.ds(first, half)]
            return pltpu.make_async_remote_copy(
                src_ref=block, dst_ref=block, send_sem=y_send.at[j, k],
                recv_sem=y_recv.at[j, k], device_id=to, device_id_type=MESH,
            )

        lo = ((s + 3) % 4) * nb
        hi = ((s + 1) % 4) * nb
        sends = [cp(0, own, right), cp(1, own + half, left), cp(2, own + half, right), cp(3, own, left)]
        forwards = [cp(4, lo, right), cp(5, hi + half, left)]
        return sends, forwards

    def send_own(j, later=None):
        sends = y_copies(j)[0]
        sends[0].start()
        sends[1].start()
        if later is not None:
            forward(later)
        sends[2].start()
        sends[3].start()

    def forward(j):
        sends, forwards = y_copies(j)
        for k in range(2):
            sends[k].wait_recv()
            forwards[k].start()

    def xz_copies(j):
        out = outs[(j // NC) % 2][j % NC]
        block = out.at[pl.ds(base, offered)]
        return [
            pltpu.make_async_remote_copy(
                src_ref=block, dst_ref=block, send_sem=xz_send.at[j], recv_sem=xz_recv.at[j],
                device_id=dev(dz, dx, 0, 0), device_id_type=MESH,
            )
            for dz, dx in plane
        ]

    def wait_bytes(out, sem):
        view = out.at[pl.ds(0, len(plane) * offered)]
        pltpu.make_async_copy(view, view, sem).wait()

    def export(j):
        sends, forwards = y_copies(j)
        sends[2].wait_recv()
        sends[3].wait_recv()
        for cp in forwards:
            cp.wait_recv()
        for cp in sends:
            cp.wait_send()
        part = parts[(j // NC) % 2][j % NC]
        out = outs[(j // NC) % 2][j % NC]
        if j < NC:

            def one(k, carry):
                part[k] = (raws[j][k].astype(F32) * dall[pl.ds(k, 1), :]).astype(BF16)
                return carry

            lax.fori_loop(0, 4 * nb, one, 0, unroll=8)
        for e in range(offered):
            out[base + e] = part[exp_ref[e]]
        for cp in xz_copies(j):
            cp.start()

    def core_copy(j):
        block = outs[(j // NC) % 2][j % NC].at[pl.ds(core * (16 * offered), 16 * offered)]
        return pltpu.make_async_remote_copy(
            src_ref=block, dst_ref=block, send_sem=core_send.at[j], recv_sem=core_recv.at[j],
            device_id=partner, device_id_type=MESH,
        )

    def share(j):
        out = outs[(j // NC) % 2][j % NC]
        wait_bytes(out, xz_recv.at[j])
        core_copy(j).start()
        wait_bytes(out, xz_send.at[j])
        for cp in y_copies(j)[1]:
            cp.wait_send()

    def inner(j, first, last):
        part, c = parts[(j // NC) % 2][j % NC], j % NC

        def one(b, carry):
            v = jnp.concatenate([part[ic[t, b]] for t in range(tp_in)], axis=1)
            acc[c, b] = jnp.dot(v, tin[b].reshape(tp_in * tile, tile), preferred_element_type=F32)
            return carry

        lax.fori_loop(first, last, one, 0, unroll=8)

    def scale(part, c, b, new):
        part[own + b] = (new * dinv[b, :1, :]).astype(BF16)

    def outer(j):
        n, c = j // NC, j % NC
        core_copy(j).wait_recv()
        core_copy(j).wait_send()
        out = outs[n % 2][c]
        rows = pl.ds(c * kc, kc)
        p = (n + 1) % 2

        def one(b, carry):
            v = jnp.concatenate([out[oidx[t, b]] for t in range(tp_out)], axis=1)
            o = acc[c, b] + jnp.dot(v, tout[b].reshape(tp_out * tile, tile), preferred_element_type=F32)
            new = o * rowf[b, :1, :]
            if n in (1, 2):
                new = 2.0 * new - vec[p, b, rows, :]
            vec[p, b, rows, :] = new
            if n + 1 < OPS:
                scale(parts[p][c], c, b, new)
            return carry

        lax.fori_loop(0, nb, one, 0, unroll=8)

    fslot = OPS % 2 ^ 1
    group = 4

    def wide(slot, i, rows):
        return jnp.concatenate([vec[slot, i * group + k, rows, :] for k in range(group)], axis=1)

    def product(slot):
        def one(i, carry):
            return carry + nt(wide(slot, i, slice(None)), wide(fslot, i, slice(None)))

        zero = jnp.zeros((width, width), F32)
        return lax.fori_loop(0, nb // group, one, zero)

    def rayleigh(j):
        rows = pl.ds((j % NC) * kc, kc)

        def one(i, carry):
            return carry + nt(wide(1 - fslot, i, rows), wide(fslot, i, slice(None)))

        ray[rows, :] = lax.fori_loop(0, nb // group, one, jnp.zeros((kc, width), F32))

    def spread(use, k):
        buf = (near, far)[k].at[use]
        if k == 0:
            block = buf.at[core * 4 + s]
            peers = [dev(0, 0, dy, dc) for dy in range(4) for dc in range(2) if (dy, dc) != (0, 0)]
        else:
            block = buf.at[z * 4 + x]
            peers = [dev(dz, dx, 0, 0) for dz, dx in plane]
        return [
            pltpu.make_async_remote_copy(
                src_ref=block, dst_ref=block, send_sem=sum_send.at[use, k], recv_sem=sum_recv.at[use, k],
                device_id=to, device_id_type=MESH,
            )
            for to in peers
        ]

    def sum_start(use, k, value):
        if k == 0:
            near[use, core * 4 + s] = value
        else:
            far[use, z * 4 + x] = value
        for cp in spread(use, k):
            cp.start()

    def sum_end(use, k):
        n = (8, 16)[k]
        buf = (near, far)[k].at[use]
        view = buf.at[pl.ds(0, n - 1)]
        pltpu.make_async_copy(view, view, sum_recv.at[use, k]).wait()
        pltpu.make_async_copy(view, view, sum_send.at[use, k]).wait()
        values = [buf[i] for i in range(n)]
        while len(values) > 1:
            values = [a + b for a, b in zip(values[::2], values[1::2])]
        return values[0]

    low = width // 2

    def pack(square):
        return jnp.concatenate([square[:low], square[low:]], axis=1)

    def unpack(packed):
        return jnp.concatenate([packed[:, :width], packed[:, width:]], axis=0)

    lane = lax.broadcasted_iota(jnp.int32, (1, 2 * width), 1)
    line = lax.broadcasted_iota(jnp.int32, (width, 1), 0)

    def eliminate(first, last):
        def one(k, carry):
            m = mat[...]
            row = mat[pl.ds(k, 1), :]
            inv = 1.0 / jnp.sqrt(jnp.sum(jnp.where(lane == k, row, 0.0), axis=1, keepdims=True))
            row = row * inv
            col = jnp.sum(jnp.where(lane == k, m, 0.0), axis=1, keepdims=True) * inv
            mat[...] = jnp.where(line > k, m - col * row, jnp.where(line == k, row, m))
            return carry

        lax.fori_loop(first, last, one, 0)

    def start_elimination(gram):
        eye = jnp.where(lane - width == line, 1.0, 0.0)
        gram = unpack(gram) / rows_total
        mat[...] = jnp.where(lane < width, jnp.concatenate([gram, gram], axis=1), eye)

    stages = OPS * NC

    def has(j):
        return 0 <= j < stages

    start_copy.wait()
    for b in range(nb):
        for c in range(NC):
            raws[c][own + b] = start_ref[c * kc : (c + 1) * kc, b * tile : (b + 1) * tile]
    pl.semaphore_wait(barrier, len(friends))
    send_own(0)
    for cp in table_copies:
        cp.wait()
    degrees(0, 3)
    send_own(1, 0)
    degrees(3, 6)
    send_own(2, 1)
    degrees(6, pieces)
    for cp in degree_copies():
        cp.start()
    send_own(3, 2)
    degrees_end()
    for i in range(2, stages + NC):
        if has(i - 4):
            outer(i - 4)
        if i - 4 >= stages - NC:
            rayleigh(i - 4)
        if i >= NC and has(i):
            send_own(i, i - 1)
        if i == stages:
            forward(i - 1)
        if i == stages - 1:
            sum_start(0, 0, pack(product(fslot)))
        if has(i - 2):
            export(i - 2)
            if i == 2:
                lax.fori_loop(0, nb * tp_out, slot_of, 0)
                for b in range(nb):
                    vec[0, b] = start_ref[:, b * tile : (b + 1) * tile].astype(F32)
            inner(i - 2, 0, nb // 2)
        if i == stages + 2:
            eliminate(16, 40)
        if has(i - 3):
            share(i - 3)
        if has(i - 2):
            inner(i - 2, nb // 2, nb)
        if i == stages:
            sum_start(0, 1, sum_end(0, 0))
        if i == stages + 1:
            start_elimination(sum_end(0, 1))
            eliminate(0, 16)
        if i == stages + 2:
            eliminate(40, width)

    sum_start(1, 0, pack(ray[...]))
    linv = mat[...][:, width:]
    columns = group * tile

    def basis(first, last):
        for i in range(first, last):
            view = pl.ds(i * columns, columns)
            basis_vmem[:, view] = jnp.dot(
                linv, wide(fslot, i, slice(None)), precision=HIGHEST, preferred_element_type=F32
            )
            basis_copy(i).start()

    def basis_copy(i):
        view = pl.ds(i * columns, columns)
        return pltpu.make_async_copy(basis_vmem.at[:, view], basis_ref.at[:, view], basis_sem.at[i])

    groups = nb // group
    basis(0, groups // 2)
    sum_start(1, 1, sum_end(1, 0))
    basis(groups // 2, groups)
    rayleigh_t = unpack(sum_end(1, 1)) / rows_total
    proj_ref[...] = nt(nt(linv, rayleigh_t), linv)
    for i in range(groups):
        basis_copy(i).wait()


def body(start_block, tiles_in, tiles_out, in_cols, out_cols, export_list, recv_list):
    width, local_rows = start_block.shape
    nb, tp_in, tile, _ = tiles_in.shape
    tp_out = tiles_out.shape[1]
    count = (tp_in + tp_out) * tile
    devices = lax.axis_size("dom") * lax.axis_size("sub")
    kc = width // NC
    stages = OPS * NC
    blocks = nb * 4
    slots = recv_list.size
    hbm = pl.BlockSpec(memory_space=pl.ANY)
    vmem = pl.BlockSpec(memory_space=pltpu.VMEM)
    dma = pltpu.SemaphoreType.DMA
    return pl.pallas_call(
        functools.partial(
            kernel, local_rows * devices, 1.0 / (1.25 * math.sqrt(count)), count
        ),
        out_shape=(
            jax.ShapeDtypeStruct((width, local_rows), F32),
            jax.ShapeDtypeStruct((width, width), F32),
        ),
        in_specs=[hbm] * 7,
        out_specs=(hbm, vmem),
        scratch_shapes=[
            pltpu.VMEM(start_block.shape, BF16),
            pltpu.VMEM(tiles_in.shape, BF16),
            pltpu.VMEM(tiles_out.shape, BF16),
            *[pltpu.VMEM((blocks, kc, tile), BF16) for _ in range(3 * NC)],
            *[pltpu.VMEM((slots, kc, tile), BF16) for _ in range(2 * NC)],
            pltpu.VMEM((2, nb, width, tile), F32),
            pltpu.VMEM((NC, nb, kc, tile), F32),
            pltpu.VMEM((nb, 8, tile), F32),
            pltpu.VMEM((nb, 8, tile), F32),
            pltpu.VMEM((blocks, tile), F32),
            pltpu.SMEM((tp_in, nb), jnp.int32),
            pltpu.SMEM((tp_out, nb), jnp.int32),
            pltpu.SMEM((export_list.size,), jnp.int32),
            pltpu.SMEM(recv_list.shape[:1:-1], jnp.int32),
            pltpu.SMEM((tp_out, nb), jnp.int32),
            pltpu.VMEM((width, 2 * width), F32),
            pltpu.VMEM((width, width), F32),
            pltpu.VMEM((2, 8, width // 2, 2 * width), F32),
            pltpu.VMEM((2, 16, width // 2, 2 * width), F32),
            pltpu.VMEM((width, local_rows), F32),
            dma((4,)),
            dma,
            dma((8, 2)),
            dma,
            dma,
            dma((stages, 6)),
            dma((stages, 6)),
            dma((stages,)),
            dma((stages,)),
            dma((stages,)),
            dma((stages,)),
            dma((2, 2)),
            dma((2, 2)),
            dma((8,)),
        ],
        compiler_params=pltpu.CompilerParams(
            collective_id=0, has_side_effects=True, vmem_limit_bytes=60 << 20
        ),
        name="filtered_step",
    )(
        start_block, tiles_in, tiles_out, in_cols.T, out_cols.T,
        export_list.reshape(-1), recv_list[0, 0].T,
    )


def solution(mesh):
    return jax.shard_map(
        body,
        mesh=mesh,
        in_specs=(
            P(None, ("dom", "sub")),
            P(("dom", "sub"), None, None, None),
            P(("dom", "sub"), None, None, None),
            P(("dom", "sub"), None),
            P(("dom", "sub"), None),
            P("dom", "sub", None),
            P("dom", "sub", None, None),
        ),
        out_specs=(P(None, ("dom", "sub")), P()),
        check_vma=False,
    )
```

```python
import functools
import math

import jax
import jax.numpy as jnp
from jax import lax
from jax.experimental import pallas as pl
from jax.experimental.pallas import tpu as pltpu
from jax.sharding import PartitionSpec as P

MESH = pl.DeviceIdType.MESH
HIGHEST = lax.Precision.HIGHEST
F32 = jnp.float32
BF16 = jnp.bfloat16
OPS = 4
NC = 4


def nt(a, b):
    return lax.dot_general(
        a, b, (((1,), (1,)), ((), ())), precision=HIGHEST, preferred_element_type=F32
    )


def mul(a, b):
    return jnp.dot(a, b, preferred_element_type=F32)


def mul_nt(a, b):
    return lax.dot_general(a, b, (((1,), (1,)), ((), ())), preferred_element_type=F32)


def split(value):
    high = value.astype(BF16)
    return high, (value - high.astype(F32)).astype(BF16)


def kernel(
    rows_total, spectral, count,
    start_hbm, tin_hbm, tout_hbm, ic_hbm, oc_hbm, exp_hbm, recv_hbm,
    basis_ref, proj_ref,
    start_ref, tin, tout, *scratch,
):
    raws = scratch[:NC]
    scratch = scratch[NC:]
    parts = [scratch[NC * p : NC * p + NC] for p in range(2)]
    scratch = scratch[2 * NC :]
    outs = [scratch[NC * p : NC * p + NC] for p in range(2)]
    (vec, acc, dinv, rowf, dall, ic, oc, exp_ref, recv_ref, oidx, fil_high, fil_low, image, mat, ray, near, far, basis_vmem,
     table_sem, start_sem, load_sem, d_send, d_recv, y_send, y_recv, xz_send, xz_recv, core_send, core_recv,
     sum_send, sum_recv, basis_sem) = scratch[2 * NC :]
    width = start_ref.shape[0]
    kc = width // NC
    nb, tp_in = tin.shape[:2]
    tp_out = tout.shape[1]
    tile = tin.shape[2]
    half = nb // 2
    offered = exp_hbm.shape[0]

    dom = lax.axis_index("dom")
    s = lax.axis_index("sub")
    z, x, core = dom // 8, (dom // 2) % 4, dom % 2

    def dev(dz, dx, dy, dc):
        zz, xx, cc = (z + dz) % 4, (x + dx) % 4, (core + dc) % 2
        return (zz * 8 + xx * 2 + cc, (s + dy) % 4)

    plane = [(dz, dx) for dz in range(4) for dx in range(4) if (dz, dx) != (0, 0)]
    plane.sort(key=lambda d: -min(d[0], 4 - d[0]) - min(d[1], 4 - d[1]))
    right, left, partner = dev(0, 0, 1, 0), dev(0, 0, 3, 0), dev(0, 0, 0, 1)

    barrier = pltpu.get_barrier_semaphore()
    friends = [dev(dz, dx, 0, 0) for dz, dx in plane]
    friends += [dev(0, 0, dy, dc) for dy in range(4) for dc in range(2) if (dy, dc) != (0, 0)]
    for f in friends:
        pl.semaphore_signal(barrier, inc=1, device_id=f, device_id_type=MESH)

    start_copy = pltpu.make_async_copy(start_hbm, start_ref, start_sem)
    start_copy.start()
    pieces = load_sem.shape[0]
    step = nb // pieces
    loads = []
    for i in range(pieces):
        rows = pl.ds(i * step, step)
        a = pltpu.make_async_copy(tin_hbm.at[rows], tin.at[rows], load_sem.at[i, 0])
        b = pltpu.make_async_copy(tout_hbm.at[rows], tout.at[rows], load_sem.at[i, 1])
        a.start()
        b.start()
        loads.append((a, b))

    own = s * nb
    table_copies = [
        pltpu.make_async_copy(a, b, table_sem.at[i])
        for i, (a, b) in enumerate(((ic_hbm, ic), (oc_hbm, oc), (exp_hbm, exp_ref), (recv_hbm, recv_ref)))
    ]
    for cp in table_copies:
        cp.start()

    def slot_of(i, carry):
        b, t = i // tp_out, i % tp_out
        v = oc[t, b]
        g, e = v // offered, v % offered
        oidx[t, b] = (g % 2) * (16 * offered) + (g // 2) * offered + recv_ref[e, g]
        return carry

    def total(ref, b, n):
        a = jnp.abs(ref[b].reshape(n * tile, tile)).astype(F32)
        return jnp.sum(a.reshape(n * tile // 8, 8, tile), axis=0)

    def degrees(first, last):
        for i in range(first, last):
            for cp in loads[i]:
                cp.wait()

            def degree(b, carry):
                mag = jnp.sum(total(tin, b, tp_in) + total(tout, b, tp_out), axis=0, keepdims=True)
                inv = 1.0 / jnp.sqrt(mag / count + 1e-06)
                dall[pl.ds(own + b, 1), :] = inv
                dinv[b] = jnp.broadcast_to(inv, (8, tile))
                rowf[b] = jnp.broadcast_to(spectral * inv, (8, tile))
                return carry

            lax.fori_loop(i * step, (i + 1) * step, degree, 0, unroll=True)

    def degree_copies():
        block = dall.at[pl.ds(own, nb)]
        return [
            pltpu.make_async_remote_copy(
                src_ref=block, dst_ref=block, send_sem=d_send, recv_sem=d_recv,
                device_id=dev(0, 0, d, 0), device_id_type=MESH,
            )
            for d in (1, 2, 3)
        ]

    def degrees_end():
        view = dall.at[pl.ds(0, 3 * nb)]
        pltpu.make_async_copy(view, view, d_recv).wait()
        pltpu.make_async_copy(view, view, d_send).wait()

    base = core * (16 * offered) + (z * 4 + x) * offered

    def y_copies(j):
        part = raws[j] if j < NC else parts[(j // NC) % 2][j % NC]

        def cp(k, first, to):
            block = part.at[pl.ds(first, half)]
            return pltpu.make_async_remote_copy(
                src_ref=block, dst_ref=block, send_sem=y_send.at[j, k],
                recv_sem=y_recv.at[j, k], device_id=to, device_id_type=MESH,
            )

        lo = ((s + 3) % 4) * nb
        hi = ((s + 1) % 4) * nb
        sends = [cp(0, own, right), cp(1, own + half, left), cp(2, own + half, right), cp(3, own, left)]
        forwards = [cp(4, lo, right), cp(5, hi + half, left)]
        return sends, forwards

    def send_own(j, later=None):
        sends = y_copies(j)[0]
        sends[0].start()
        sends[1].start()
        if later is not None:
            forward(later)
        sends[2].start()
        sends[3].start()

    def forward(j):
        sends, forwards = y_copies(j)
        for k in range(2):
            sends[k].wait_recv()
            forwards[k].start()

    def xz_copies(j):
        out = outs[(j // NC) % 2][j % NC]
        block = out.at[pl.ds(base, offered)]
        return [
            pltpu.make_async_remote_copy(
                src_ref=block, dst_ref=block, send_sem=xz_send.at[j], recv_sem=xz_recv.at[j, (4 - dz) % 4],
                device_id=dev(dz, dx, 0, 0), device_id_type=MESH,
            )
            for dz, dx in plane
        ]

    def wait_bytes(out, sem, n):
        view = out.at[pl.ds(0, n * offered)]
        pltpu.make_async_copy(view, view, sem).wait()

    def export(j):
        sends, forwards = y_copies(j)
        sends[2].wait_recv()
        sends[3].wait_recv()
        for cp in forwards:
            cp.wait_recv()
        for cp in sends:
            cp.wait_send()
        part = parts[(j // NC) % 2][j % NC]
        out = outs[(j // NC) % 2][j % NC]
        if j < NC:

            def one(k, carry):
                part[k] = (raws[j][k].astype(F32) * dall[pl.ds(k, 1), :]).astype(BF16)
                return carry

            lax.fori_loop(0, 4 * nb, one, 0, unroll=8)
        for e in range(offered):
            out[base + e] = part[exp_ref[e]]
        for cp in xz_copies(j):
            cp.start()

    def core_copy(j, dz):
        row = core * (16 * offered) + ((z + dz) % 4) * (4 * offered)
        block = outs[(j // NC) % 2][j % NC].at[pl.ds(row, 4 * offered)]
        return pltpu.make_async_remote_copy(
            src_ref=block, dst_ref=block, send_sem=core_send.at[j, dz], recv_sem=core_recv.at[j, dz],
            device_id=partner, device_id_type=MESH,
        )

    def share(j):
        out = outs[(j // NC) % 2][j % NC]
        for dz in (0, 1, 3, 2):
            wait_bytes(out, xz_recv.at[j, dz], 3 if dz == 0 else 4)
            core_copy(j, dz).start()
        wait_bytes(out, xz_send.at[j], len(plane))
        for cp in y_copies(j)[1]:
            cp.wait_send()

    def inner(j, first, last):
        part, c = parts[(j // NC) % 2][j % NC], j % NC

        def one(b, carry):
            v = jnp.concatenate([part[ic[t, b]] for t in range(tp_in)], axis=1)
            acc[c, b] = jnp.dot(v, tin[b].reshape(tp_in * tile, tile), preferred_element_type=F32)
            return carry

        lax.fori_loop(first, last, one, 0, unroll=8)

    def scale(part, c, b, new):
        part[own + b] = (new * dinv[b, :1, :]).astype(BF16)

    def outer(j):
        n, c = j // NC, j % NC
        for dz in range(4):
            core_copy(j, dz).wait_recv()
            core_copy(j, dz).wait_send()
        out = outs[n % 2][c]
        rows = pl.ds(c * kc, kc)
        p = (n + 1) % 2

        def one(b, carry):
            v = jnp.concatenate([out[oidx[t, b]] for t in range(tp_out)], axis=1)
            o = acc[c, b] + jnp.dot(v, tout[b].reshape(tp_out * tile, tile), preferred_element_type=F32)
            new = o * rowf[b, :1, :]
            columns = pl.ds(pl.multiple_of(b * tile, tile), tile)
            if n == 0:
                vec[b, rows, :] = new
            elif n == 1:
                new = 2.0 * new - start_ref[rows, columns].astype(F32)
            elif n == 2:
                new = 2.0 * new - vec[b, rows, :]
                fil_high[rows, columns], fil_low[rows, columns] = split(new)
            else:
                image[:kc, columns], image[kc:, columns] = split(new)
            if n + 1 < OPS:
                scale(parts[p][c], c, b, new)
            return carry

        lax.fori_loop(0, nb, one, 0, unroll=8)

    def product():
        high = fil_high[...]
        both = mul_nt(high, jnp.concatenate([high, fil_low[...]], axis=0))
        return both[:, :width] + both[:, width:] + mul_nt(fil_low[...], high)

    def rayleigh(j):
        both = mul_nt(image[...], fil_high[...])
        got = both[:kc] + both[kc:] + mul_nt(image[:kc, :], fil_low[...])
        ray[pl.ds((j % NC) * kc, kc), :] = got

    def spread(use, k):
        buf = (near, far)[k].at[use]
        if k == 0:
            block = buf.at[core * 4 + s]
            peers = [dev(0, 0, dy, dc) for dy in range(4) for dc in range(2) if (dy, dc) != (0, 0)]
        else:
            block = buf.at[z * 4 + x]
            peers = [dev(dz, dx, 0, 0) for dz, dx in plane]
        return [
            pltpu.make_async_remote_copy(
                src_ref=block, dst_ref=block, send_sem=sum_send.at[use, k], recv_sem=sum_recv.at[use, k],
                device_id=to, device_id_type=MESH,
            )
            for to in peers
        ]

    def sum_start(use, k, value):
        if k == 0:
            near[use, core * 4 + s] = value
        else:
            far[use, z * 4 + x] = value
        for cp in spread(use, k):
            cp.start()

    def sum_end(use, k):
        n = (8, 16)[k]
        buf = (near, far)[k].at[use]
        view = buf.at[pl.ds(0, n - 1)]
        pltpu.make_async_copy(view, view, sum_recv.at[use, k]).wait()
        pltpu.make_async_copy(view, view, sum_send.at[use, k]).wait()
        values = [buf[i] for i in range(n)]
        while len(values) > 1:
            values = [a + b for a, b in zip(values[::2], values[1::2])]
        return values[0]

    low = width // 2

    def pack(square):
        return jnp.concatenate([square[:low], square[low:]], axis=1)

    def unpack(packed):
        return jnp.concatenate([packed[:, :width], packed[:, width:]], axis=0)

    lane = lax.broadcasted_iota(jnp.int32, (1, 2 * width), 1)
    line = lax.broadcasted_iota(jnp.int32, (width, 1), 0)

    def eliminate(first, last):
        def one(k, carry):
            m = mat[...]
            row = mat[pl.ds(k, 1), :]
            inv = 1.0 / jnp.sqrt(jnp.sum(jnp.where(lane == k, row, 0.0), axis=1, keepdims=True))
            row = row * inv
            col = jnp.sum(jnp.where(lane == k, m, 0.0), axis=1, keepdims=True) * inv
            mat[...] = jnp.where(line > k, m - col * row, jnp.where(line == k, row, m))
            return carry

        lax.fori_loop(first, last, one, 0)

    def start_elimination(gram):
        eye = jnp.where(lane - width == line, 1.0, 0.0)
        gram = unpack(gram) / rows_total
        mat[...] = jnp.where(lane < width, jnp.concatenate([gram, gram], axis=1), eye)

    stages = OPS * NC

    def has(j):
        return 0 <= j < stages

    start_copy.wait()
    for b in range(nb):
        for c in range(NC):
            raws[c][own + b] = start_ref[c * kc : (c + 1) * kc, b * tile : (b + 1) * tile]
    pl.semaphore_wait(barrier, len(friends))
    send_own(0)
    for cp in table_copies:
        cp.wait()
    degrees(0, 3)
    send_own(1, 0)
    degrees(3, 6)
    send_own(2, 1)
    degrees(6, pieces)
    for cp in degree_copies():
        cp.start()
    send_own(3, 2)
    lax.fori_loop(0, nb * tp_out, slot_of, 0, unroll=8)
    degrees_end()
    for i in range(2, stages + NC):
        if has(i - 4):
            outer(i - 4)
        if i - 4 >= stages - NC:
            rayleigh(i - 4)
        if i >= NC and has(i):
            send_own(i, i - 1)
        if i == stages:
            forward(i - 1)
        if i == stages - 1:
            sum_start(0, 0, pack(product()))
        if has(i - 2):
            export(i - 2)
            inner(i - 2, 0, nb // 2)
        if has(i - 3):
            share(i - 3)
        if has(i - 2):
            inner(i - 2, nb // 2, nb)
        if i == stages - 1:
            sum_start(0, 1, sum_end(0, 0))

    sum_start(1, 0, pack(ray[...]))
    start_elimination(sum_end(0, 1))
    eliminate(0, 40)
    sum_start(1, 1, sum_end(1, 0))
    eliminate(40, width)
    linv = mat[...][:, width:]
    linv_high, linv_low = split(linv)
    linv_both = jnp.concatenate([linv_high, linv_low], axis=0)
    columns = 4 * tile

    def basis(first, last):
        for i in range(first, last):
            view = pl.ds(i * columns, columns)
            both = mul(linv_both, fil_high[:, view])
            basis_vmem[:, view] = both[:width] + both[width:] + mul(linv_high, fil_low[:, view])
            basis_copy(i).start()

    def basis_copy(i):
        view = pl.ds(i * columns, columns)
        return pltpu.make_async_copy(basis_vmem.at[:, view], basis_ref.at[:, view], basis_sem.at[i])

    groups = nb // 4
    basis(0, groups)
    rayleigh_t = unpack(sum_end(1, 1)) / rows_total
    proj_ref[...] = nt(nt(linv, rayleigh_t), linv)
    for i in range(groups):
        basis_copy(i).wait()


def deliver(basis, proj, basis_out, proj_out, held, held_proj, sem):
    width = basis.shape[1] // 4
    steps = []
    for i in range(5):
        if i < 4:
            part = (slice(None), pl.ds(i * width, width))
            refs = basis.at[part], held.at[part], basis_out.at[part]
        else:
            refs = proj, held_proj, proj_out
        steps.append(
            (pltpu.make_async_copy(refs[0], refs[1], sem.at[i, 0]),
             pltpu.make_async_copy(refs[1], refs[2], sem.at[i, 1]))
        )
    for come, _ in steps:
        come.start()
    for come, go in steps:
        come.wait()
        go.start()
    for _, go in steps:
        go.wait()


def body(start_block, tiles_in, tiles_out, in_cols, out_cols, export_list, recv_list):
    width, local_rows = start_block.shape
    nb, tp_in, tile, _ = tiles_in.shape
    tp_out = tiles_out.shape[1]
    count = (tp_in + tp_out) * tile
    devices = lax.axis_size("dom") * lax.axis_size("sub")
    kc = width // NC
    stages = OPS * NC
    blocks = nb * 4
    slots = recv_list.size
    hbm = pl.BlockSpec(memory_space=pl.ANY)
    vmem = pl.BlockSpec(memory_space=pltpu.VMEM)
    dma = pltpu.SemaphoreType.DMA
    outputs = pl.pallas_call(
        functools.partial(
            kernel, local_rows * devices, 1.0 / (1.25 * math.sqrt(count)), count
        ),
        out_shape=(
            jax.ShapeDtypeStruct((width, local_rows), F32),
            jax.ShapeDtypeStruct((width, width), F32),
        ),
        in_specs=[hbm] * 7,
        out_specs=(hbm, vmem),
        scratch_shapes=[
            pltpu.VMEM(start_block.shape, BF16),
            pltpu.VMEM(tiles_in.shape, BF16),
            pltpu.VMEM(tiles_out.shape, BF16),
            *[pltpu.VMEM((blocks, kc, tile), BF16) for _ in range(3 * NC)],
            *[pltpu.VMEM((slots, kc, tile), BF16) for _ in range(2 * NC)],
            pltpu.VMEM((nb, width, tile), F32),
            pltpu.VMEM((NC, nb, kc, tile), F32),
            pltpu.VMEM((nb, 8, tile), F32),
            pltpu.VMEM((nb, 8, tile), F32),
            pltpu.VMEM((blocks, tile), F32),
            pltpu.SMEM((tp_in, nb), jnp.int32),
            pltpu.SMEM((tp_out, nb), jnp.int32),
            pltpu.SMEM((export_list.size,), jnp.int32),
            pltpu.SMEM(recv_list.shape[:1:-1], jnp.int32),
            pltpu.SMEM((tp_out, nb), jnp.int32),
            pltpu.VMEM((width, local_rows), BF16),
            pltpu.VMEM((width, local_rows), BF16),
            pltpu.VMEM((2 * kc, local_rows), BF16),
            pltpu.VMEM((width, 2 * width), F32),
            pltpu.VMEM((width, width), F32),
            pltpu.VMEM((2, 8, width // 2, 2 * width), F32),
            pltpu.VMEM((2, 16, width // 2, 2 * width), F32),
            pltpu.VMEM((width, local_rows), F32),
            dma((4,)),
            dma,
            dma((8, 2)),
            dma,
            dma,
            dma((stages, 6)),
            dma((stages, 6)),
            dma((stages,)),
            dma((stages, 4)),
            dma((stages, 4)),
            dma((stages, 4)),
            dma((2, 2)),
            dma((2, 2)),
            dma((8,)),
        ],
        compiler_params=pltpu.CompilerParams(
            collective_id=0, has_side_effects=True, vmem_limit_bytes=60 << 20
        ),
        name="filtered_step",
    )(
        start_block, tiles_in, tiles_out, in_cols.T, out_cols.T,
        export_list.reshape(-1), recv_list[0, 0].T,
    )
    return pl.pallas_call(
        deliver,
        out_shape=tuple(jax.ShapeDtypeStruct(o.shape, o.dtype) for o in outputs),
        in_specs=[hbm, hbm],
        out_specs=(hbm, hbm),
        scratch_shapes=[*[pltpu.VMEM(o.shape, o.dtype) for o in outputs], dma((5, 2))],
        compiler_params=pltpu.CompilerParams(vmem_limit_bytes=60 << 20),
        name="deliver",
    )(*outputs)


def solution(mesh):
    return jax.shard_map(
        body,
        mesh=mesh,
        in_specs=(
            P(None, ("dom", "sub")),
            P(("dom", "sub"), None, None, None),
            P(("dom", "sub"), None, None, None),
            P(("dom", "sub"), None),
            P(("dom", "sub"), None),
            P("dom", "sub", None),
            P("dom", "sub", None, None),
        ),
        out_specs=(P(None, ("dom", "sub")), P()),
        check_vma=False,
    )
```

```python
import functools
import math

import jax
import jax.numpy as jnp
from jax import lax
from jax.experimental import pallas as pl
from jax.experimental.pallas import tpu as pltpu
from jax.sharding import PartitionSpec as P

MESH = pl.DeviceIdType.MESH
HIGHEST = lax.Precision.HIGHEST
F32 = jnp.float32
BF16 = jnp.bfloat16
OPS = 4
NC = 4


def nt(a, b):
    return lax.dot_general(
        a, b, (((1,), (1,)), ((), ())), precision=HIGHEST, preferred_element_type=F32
    )


def mul(a, b):
    return jnp.dot(a, b, preferred_element_type=F32)


def mul_nt(a, b):
    return lax.dot_general(a, b, (((1,), (1,)), ((), ())), preferred_element_type=F32)


def split(value):
    high = value.astype(BF16)
    return high, (value - high.astype(F32)).astype(BF16)


def kernel(
    rows_total, spectral, count,
    start_hbm, tin_hbm, tout_hbm, ic_hbm, oc_hbm, exp_hbm, recv_hbm,
    basis_ref, proj_ref,
    start_ref, tin, tout, *scratch,
):
    raws = scratch[:NC]
    scratch = scratch[NC:]
    parts = [scratch[NC * p : NC * p + NC] for p in range(2)]
    scratch = scratch[2 * NC :]
    outs = [scratch[NC * p : NC * p + NC] for p in range(2)]
    (vec, acc, dinv, rowf, dall, ic, oc, exp_ref, recv_ref, oidx, fil_high, fil_low, image, mat, ray, near, far, basis_vmem,
     table_sem, start_sem, load_sem, d_send, d_recv, y_send, y_recv, xz_send, xz_recv, core_send, core_recv,
     sum_send, sum_recv, basis_sem) = scratch[2 * NC :]
    width = start_ref.shape[0]
    kc = width // NC
    nb, tp_in = tin.shape[:2]
    tp_out = tout.shape[1]
    tile = tin.shape[2]
    half = nb // 2
    offered = exp_hbm.shape[0]

    dom = lax.axis_index("dom")
    s = lax.axis_index("sub")
    z, x, core = dom // 8, (dom // 2) % 4, dom % 2

    def dev(dz, dx, dy, dc):
        zz, xx, cc = (z + dz) % 4, (x + dx) % 4, (core + dc) % 2
        return (zz * 8 + xx * 2 + cc, (s + dy) % 4)

    plane = [(dz, dx) for dz in range(4) for dx in range(4) if (dz, dx) != (0, 0)]
    plane.sort(key=lambda d: -min(d[0], 4 - d[0]) - min(d[1], 4 - d[1]))
    right, left, partner = dev(0, 0, 1, 0), dev(0, 0, 3, 0), dev(0, 0, 0, 1)

    barrier = pltpu.get_barrier_semaphore()
    friends = [dev(dz, dx, 0, 0) for dz, dx in plane]
    friends += [dev(0, 0, dy, dc) for dy in range(4) for dc in range(2) if (dy, dc) != (0, 0)]
    for f in friends:
        pl.semaphore_signal(barrier, inc=1, device_id=f, device_id_type=MESH)

    start_copy = pltpu.make_async_copy(start_hbm, start_ref, start_sem)
    start_copy.start()
    pieces = load_sem.shape[0]
    step = nb // pieces
    loads = []
    for i in range(pieces):
        rows = pl.ds(i * step, step)
        a = pltpu.make_async_copy(tin_hbm.at[rows], tin.at[rows], load_sem.at[i, 0])
        b = pltpu.make_async_copy(tout_hbm.at[rows], tout.at[rows], load_sem.at[i, 1])
        a.start()
        b.start()
        loads.append((a, b))

    own = s * nb
    table_copies = [
        pltpu.make_async_copy(a, b, table_sem.at[i])
        for i, (a, b) in enumerate(((ic_hbm, ic), (oc_hbm, oc), (exp_hbm, exp_ref), (recv_hbm, recv_ref)))
    ]
    for cp in table_copies:
        cp.start()

    def slot_of(i, carry):
        b, t = i // tp_out, i % tp_out
        v = oc[t, b]
        g, e = v // offered, v % offered
        oidx[t, b] = (g % 2) * (16 * offered) + (g // 2) * offered + recv_ref[e, g]
        return carry

    def total(ref, b, n):
        a = jnp.abs(ref[b].reshape(n * tile, tile)).astype(F32)
        return jnp.sum(a.reshape(n * tile // 8, 8, tile), axis=0)

    def degrees(first, last):
        for i in range(first, last):
            for cp in loads[i]:
                cp.wait()

            def degree(b, carry):
                mag = jnp.sum(total(tin, b, tp_in) + total(tout, b, tp_out), axis=0, keepdims=True)
                inv = 1.0 / jnp.sqrt(mag / count + 1e-06)
                dall[pl.ds(own + b, 1), :] = inv
                dinv[b] = jnp.broadcast_to(inv, (8, tile))
                rowf[b] = jnp.broadcast_to(spectral * inv, (8, tile))
                return carry

            lax.fori_loop(i * step, (i + 1) * step, degree, 0, unroll=True)

    def degree_copies():
        block = dall.at[pl.ds(own, nb)]
        return [
            pltpu.make_async_remote_copy(
                src_ref=block, dst_ref=block, send_sem=d_send, recv_sem=d_recv,
                device_id=dev(0, 0, d, 0), device_id_type=MESH,
            )
            for d in (1, 2, 3)
        ]

    def degrees_end():
        view = dall.at[pl.ds(0, 3 * nb)]
        pltpu.make_async_copy(view, view, d_recv).wait()
        pltpu.make_async_copy(view, view, d_send).wait()

    base = core * (16 * offered) + (z * 4 + x) * offered

    def y_copies(j):
        part = raws[j] if j < NC else parts[(j // NC) % 2][j % NC]

        def cp(k, first, to):
            block = part.at[pl.ds(first, half)]
            return pltpu.make_async_remote_copy(
                src_ref=block, dst_ref=block, send_sem=y_send.at[j, k],
                recv_sem=y_recv.at[j, k], device_id=to, device_id_type=MESH,
            )

        lo = ((s + 3) % 4) * nb
        hi = ((s + 1) % 4) * nb
        sends = [cp(0, own, right), cp(1, own + half, left), cp(2, own + half, right), cp(3, own, left)]
        forwards = [cp(4, lo, right), cp(5, hi + half, left)]
        return sends, forwards

    def send_own(j, which=(0, 1, 2, 3)):
        sends = y_copies(j)[0]
        for k in which:
            sends[k].start()

    def forward(j):
        sends, forwards = y_copies(j)
        for k in range(2):
            sends[k].wait_recv()
            forwards[k].start()

    def xz_copies(j):
        out = outs[(j // NC) % 2][j % NC]
        block = out.at[pl.ds(base, offered)]
        return [
            pltpu.make_async_remote_copy(
                src_ref=block, dst_ref=block, send_sem=xz_send.at[j], recv_sem=xz_recv.at[j, (4 - dz) % 4],
                device_id=dev(dz, dx, 0, 0), device_id_type=MESH,
            )
            for dz, dx in plane
        ]

    def wait_bytes(out, sem, n):
        view = out.at[pl.ds(0, n * offered)]
        pltpu.make_async_copy(view, view, sem).wait()

    def export(j):
        sends, forwards = y_copies(j)
        sends[2].wait_recv()
        sends[3].wait_recv()
        for cp in forwards:
            cp.wait_recv()
        for cp in sends:
            cp.wait_send()
        part = parts[(j // NC) % 2][j % NC]
        out = outs[(j // NC) % 2][j % NC]
        if j < NC:

            def one(k, carry):
                part[k] = (raws[j][k].astype(F32) * dall[pl.ds(k, 1), :]).astype(BF16)
                return carry

            lax.fori_loop(0, 4 * nb, one, 0, unroll=8)
        for e in range(offered):
            out[base + e] = part[exp_ref[e]]
        for cp in xz_copies(j):
            cp.start()

    def core_copy(j, dz):
        row = core * (16 * offered) + ((z + dz) % 4) * (4 * offered)
        block = outs[(j // NC) % 2][j % NC].at[pl.ds(row, 4 * offered)]
        return pltpu.make_async_remote_copy(
            src_ref=block, dst_ref=block, send_sem=core_send.at[j, dz], recv_sem=core_recv.at[j, dz],
            device_id=partner, device_id_type=MESH,
        )

    def share(j):
        out = outs[(j // NC) % 2][j % NC]
        for dz in (0, 1, 3, 2):
            wait_bytes(out, xz_recv.at[j, dz], 3 if dz == 0 else 4)
            core_copy(j, dz).start()
        wait_bytes(out, xz_send.at[j], len(plane))
        for cp in y_copies(j)[1]:
            cp.wait_send()

    def inner(j, first, last):
        part, c = parts[(j // NC) % 2][j % NC], j % NC

        def one(b, carry):
            v = jnp.concatenate([part[ic[t, b]] for t in range(tp_in)], axis=1)
            acc[c, b] = jnp.dot(v, tin[b].reshape(tp_in * tile, tile), preferred_element_type=F32)
            return carry

        lax.fori_loop(first, last, one, 0, unroll=16)

    def scale(part, c, b, new):
        part[own + b] = (new * dinv[b, :1, :]).astype(BF16)

    def shared(j):
        for dz in range(4):
            core_copy(j, dz).wait_recv()
            core_copy(j, dz).wait_send()

    def outer(j, first, last):
        n, c = j // NC, j % NC
        out = outs[n % 2][c]
        rows = pl.ds(c * kc, kc)
        p = (n + 1) % 2

        def one(b, carry):
            v = jnp.concatenate([out[oidx[t, b]] for t in range(tp_out)], axis=1)
            o = acc[c, b] + jnp.dot(v, tout[b].reshape(tp_out * tile, tile), preferred_element_type=F32)
            new = o * rowf[b, :1, :]
            columns = pl.ds(pl.multiple_of(b * tile, tile), tile)
            if n == 0:
                vec[b, rows, :] = new
            elif n == 1:
                new = 2.0 * new - start_ref[rows, columns].astype(F32)
            elif n == 2:
                new = 2.0 * new - vec[b, rows, :]
                fil_high[rows, columns], fil_low[rows, columns] = split(new)
            else:
                image[:kc, columns], image[kc:, columns] = split(new)
            if n + 1 < OPS:
                scale(parts[p][c], c, b, new)
            return carry

        lax.fori_loop(first, last, one, 0, unroll=16)

    def product():
        high = fil_high[...]
        both = mul_nt(high, jnp.concatenate([high, fil_low[...]], axis=0))
        return both[:, :width] + both[:, width:] + mul_nt(fil_low[...], high)

    def rayleigh(j):
        both = mul_nt(image[...], fil_high[...])
        got = both[:kc] + both[kc:] + mul_nt(image[:kc, :], fil_low[...])
        ray[pl.ds((j % NC) * kc, kc), :] = got

    def spread(use, k):
        buf = (near, far)[k].at[use]
        if k == 0:
            block = buf.at[core * 4 + s]
            peers = [dev(0, 0, dy, dc) for dy in range(4) for dc in range(2) if (dy, dc) != (0, 0)]
        else:
            block = buf.at[z * 4 + x]
            peers = [dev(dz, dx, 0, 0) for dz, dx in plane]
        return [
            pltpu.make_async_remote_copy(
                src_ref=block, dst_ref=block, send_sem=sum_send.at[use, k], recv_sem=sum_recv.at[use, k],
                device_id=to, device_id_type=MESH,
            )
            for to in peers
        ]

    def sum_start(use, k, value):
        if k == 0:
            near[use, core * 4 + s] = value
        else:
            far[use, z * 4 + x] = value
        for cp in spread(use, k):
            cp.start()

    def sum_end(use, k):
        n = (8, 16)[k]
        buf = (near, far)[k].at[use]
        view = buf.at[pl.ds(0, n - 1)]
        pltpu.make_async_copy(view, view, sum_recv.at[use, k]).wait()
        pltpu.make_async_copy(view, view, sum_send.at[use, k]).wait()
        values = [buf[i] for i in range(n)]
        while len(values) > 1:
            values = [a + b for a, b in zip(values[::2], values[1::2])]
        return values[0]

    low = width // 2

    def pack(square):
        return jnp.concatenate([square[:low], square[low:]], axis=1)

    def unpack(packed):
        return jnp.concatenate([packed[:, :width], packed[:, width:]], axis=0)

    lane = lax.broadcasted_iota(jnp.int32, (1, 2 * width), 1)
    line = lax.broadcasted_iota(jnp.int32, (width, 1), 0)

    def eliminate(first, last):
        def one(k, carry):
            m = mat[...]
            row = mat[pl.ds(k, 1), :]
            inv = 1.0 / jnp.sqrt(jnp.sum(jnp.where(lane == k, row, 0.0), axis=1, keepdims=True))
            row = row * inv
            col = jnp.sum(jnp.where(lane == k, m, 0.0), axis=1, keepdims=True) * inv
            mat[...] = jnp.where(line > k, m - col * row, jnp.where(line == k, row, m))
            return carry

        lax.fori_loop(first, last, one, 0)

    def start_elimination(gram):
        eye = jnp.where(lane - width == line, 1.0, 0.0)
        gram = unpack(gram) / rows_total
        mat[...] = jnp.where(lane < width, jnp.concatenate([gram, gram], axis=1), eye)

    stages = OPS * NC

    def has(j):
        return 0 <= j < stages

    start_copy.wait()
    for b in range(nb):
        for c in range(NC):
            raws[c][own + b] = start_ref[c * kc : (c + 1) * kc, b * tile : (b + 1) * tile]
    pl.semaphore_wait(barrier, len(friends))
    send_own(0)
    for cp in table_copies:
        cp.wait()
    degrees(0, 3)
    send_own(1, (0, 1))
    forward(0)
    send_own(1, (2, 3))
    degrees(3, 6)
    send_own(2, (0, 1))
    forward(1)
    send_own(2, (2, 3))
    degrees(6, pieces)
    for cp in degree_copies():
        cp.start()
    send_own(3, (0, 1))
    forward(2)
    send_own(3, (2, 3))
    lax.fori_loop(0, nb * tp_out, slot_of, 0, unroll=8)
    degrees_end()
    export(0)
    for i in range(2, stages + NC):
        if has(i - 4):
            shared(i - 4)
            outer(i - 4, 0, half)
        if i >= NC and has(i - 1):
            forward(i - 1)
        if i >= NC and has(i):
            send_own(i, (0,))
        if has(i - 4):
            outer(i - 4, half, nb)
        if i >= NC and has(i):
            send_own(i, (1, 2, 3))
        if i - 4 >= stages - NC:
            rayleigh(i - 4)
        if has(i - 3):
            share(i - 3)
        if i == stages - 1:
            sum_start(0, 0, pack(product()))
        if i == stages:
            sum_start(0, 1, sum_end(0, 0))
        if has(i - 2):
            inner(i - 2, 0, nb)
        if has(i - 1):
            export(i - 1)

    sum_start(1, 0, pack(ray[...]))
    start_elimination(sum_end(0, 1))
    eliminate(0, 40)
    sum_start(1, 1, sum_end(1, 0))
    eliminate(40, width)
    linv = mat[...][:, width:]
    linv_high, linv_low = split(linv)
    linv_both = jnp.concatenate([linv_high, linv_low], axis=0)
    columns = 4 * tile

    def basis(first, last):
        for i in range(first, last):
            view = pl.ds(i * columns, columns)
            both = mul(linv_both, fil_high[:, view])
            basis_vmem[:, view] = both[:width] + both[width:] + mul(linv_high, fil_low[:, view])
            basis_copy(i).start()

    def basis_copy(i):
        view = pl.ds(i * columns, columns)
        return pltpu.make_async_copy(basis_vmem.at[:, view], basis_ref.at[:, view], basis_sem.at[i])

    groups = nb // 4
    basis(0, groups)
    rayleigh_t = unpack(sum_end(1, 1)) / rows_total
    proj_ref[...] = nt(nt(linv, rayleigh_t), linv)
    for i in range(groups):
        basis_copy(i).wait()


def deliver(basis, proj, basis_out, proj_out, held, held_proj, sem):
    width = basis.shape[1] // 4
    steps = []
    for i in range(5):
        if i < 4:
            part = (slice(None), pl.ds(i * width, width))
            refs = basis.at[part], held.at[part], basis_out.at[part]
        else:
            refs = proj, held_proj, proj_out
        steps.append(
            (pltpu.make_async_copy(refs[0], refs[1], sem.at[i, 0]),
             pltpu.make_async_copy(refs[1], refs[2], sem.at[i, 1]))
        )
    for come, _ in steps:
        come.start()
    for come, go in steps:
        come.wait()
        go.start()
    for _, go in steps:
        go.wait()


def body(start_block, tiles_in, tiles_out, in_cols, out_cols, export_list, recv_list):
    width, local_rows = start_block.shape
    nb, tp_in, tile, _ = tiles_in.shape
    tp_out = tiles_out.shape[1]
    count = (tp_in + tp_out) * tile
    devices = lax.axis_size("dom") * lax.axis_size("sub")
    kc = width // NC
    stages = OPS * NC
    blocks = nb * 4
    slots = recv_list.size
    hbm = pl.BlockSpec(memory_space=pl.ANY)
    vmem = pl.BlockSpec(memory_space=pltpu.VMEM)
    dma = pltpu.SemaphoreType.DMA
    outputs = pl.pallas_call(
        functools.partial(
            kernel, local_rows * devices, 1.0 / (1.25 * math.sqrt(count)), count
        ),
        out_shape=(
            jax.ShapeDtypeStruct((width, local_rows), F32),
            jax.ShapeDtypeStruct((width, width), F32),
        ),
        in_specs=[hbm] * 7,
        out_specs=(hbm, vmem),
        scratch_shapes=[
            pltpu.VMEM(start_block.shape, BF16),
            pltpu.VMEM(tiles_in.shape, BF16),
            pltpu.VMEM(tiles_out.shape, BF16),
            *[pltpu.VMEM((blocks, kc, tile), BF16) for _ in range(3 * NC)],
            *[pltpu.VMEM((slots, kc, tile), BF16) for _ in range(2 * NC)],
            pltpu.VMEM((nb, width, tile), F32),
            pltpu.VMEM((NC, nb, kc, tile), F32),
            pltpu.VMEM((nb, 8, tile), F32),
            pltpu.VMEM((nb, 8, tile), F32),
            pltpu.VMEM((blocks, tile), F32),
            pltpu.SMEM((tp_in, nb), jnp.int32),
            pltpu.SMEM((tp_out, nb), jnp.int32),
            pltpu.SMEM((export_list.size,), jnp.int32),
            pltpu.SMEM(recv_list.shape[:1:-1], jnp.int32),
            pltpu.SMEM((tp_out, nb), jnp.int32),
            pltpu.VMEM((width, local_rows), BF16),
            pltpu.VMEM((width, local_rows), BF16),
            pltpu.VMEM((2 * kc, local_rows), BF16),
            pltpu.VMEM((width, 2 * width), F32),
            pltpu.VMEM((width, width), F32),
            pltpu.VMEM((2, 8, width // 2, 2 * width), F32),
            pltpu.VMEM((2, 16, width // 2, 2 * width), F32),
            pltpu.VMEM((width, local_rows), F32),
            dma((4,)),
            dma,
            dma((8, 2)),
            dma,
            dma,
            dma((stages, 6)),
            dma((stages, 6)),
            dma((stages,)),
            dma((stages, 4)),
            dma((stages, 4)),
            dma((stages, 4)),
            dma((2, 2)),
            dma((2, 2)),
            dma((8,)),
        ],
        compiler_params=pltpu.CompilerParams(
            collective_id=0, has_side_effects=True, vmem_limit_bytes=60 << 20
        ),
        name="filtered_step",
    )(
        start_block, tiles_in, tiles_out, in_cols.T, out_cols.T,
        export_list.reshape(-1), recv_list[0, 0].T,
    )
    return pl.pallas_call(
        deliver,
        out_shape=tuple(jax.ShapeDtypeStruct(o.shape, o.dtype) for o in outputs),
        in_specs=[hbm, hbm],
        out_specs=(hbm, hbm),
        scratch_shapes=[*[pltpu.VMEM(o.shape, o.dtype) for o in outputs], dma((5, 2))],
        compiler_params=pltpu.CompilerParams(vmem_limit_bytes=60 << 20),
        name="deliver",
    )(*outputs)


def solution(mesh):
    return jax.shard_map(
        body,
        mesh=mesh,
        in_specs=(
            P(None, ("dom", "sub")),
            P(("dom", "sub"), None, None, None),
            P(("dom", "sub"), None, None, None),
            P(("dom", "sub"), None),
            P(("dom", "sub"), None),
            P("dom", "sub", None),
            P("dom", "sub", None, None),
        ),
        out_specs=(P(None, ("dom", "sub")), P()),
        check_vma=False,
    )
```

```python
import functools
import math

import jax
import jax.numpy as jnp
from jax import lax
from jax.experimental import pallas as pl
from jax.experimental.pallas import tpu as pltpu
from jax.sharding import PartitionSpec as P

MESH = pl.DeviceIdType.MESH
HIGHEST = lax.Precision.HIGHEST
F32 = jnp.float32
BF16 = jnp.bfloat16
OPS = 4
NC = 4


def nt(a, b):
    return lax.dot_general(
        a, b, (((1,), (1,)), ((), ())), precision=HIGHEST, preferred_element_type=F32
    )


def mul(a, b):
    return jnp.dot(a, b, preferred_element_type=F32)


def mul_nt(a, b):
    return lax.dot_general(a, b, (((1,), (1,)), ((), ())), preferred_element_type=F32)


def split(value):
    high = value.astype(BF16)
    return high, (value - high.astype(F32)).astype(BF16)


def kernel(
    rows_total, spectral, count,
    start_hbm, tin_hbm, tout_hbm, ic_hbm, oc_hbm, exp_hbm, recv_hbm,
    basis_ref, proj_ref,
    start_ref, tin, tout, *scratch,
):
    raws = scratch[:NC]
    scratch = scratch[NC:]
    parts = [scratch[NC * p : NC * p + NC] for p in range(2)]
    scratch = scratch[2 * NC :]
    outs = [scratch[NC * p : NC * p + NC] for p in range(2)]
    (vec, acc, dinv, rowf, dall, ic, oc, exp_ref, recv_ref, oidx, fil_high, fil_low, image, mat, ray, near, far, basis_vmem,
     table_sem, start_sem, load_sem, d_send, d_recv, y_send, y_recv, xz_send, xz_recv, core_send, core_recv,
     sum_send, sum_recv, basis_sem) = scratch[2 * NC :]
    width = start_ref.shape[0]
    kc = width // NC
    nb, tp_in = tin.shape[:2]
    tp_out = tout.shape[1]
    tile = tin.shape[2]
    half = nb // 2
    offered = exp_hbm.shape[0]

    dom = lax.axis_index("dom")
    s = lax.axis_index("sub")
    z, x, core = dom // 8, (dom // 2) % 4, dom % 2

    def dev(dz, dx, dy, dc):
        zz, xx, cc = (z + dz) % 4, (x + dx) % 4, (core + dc) % 2
        return (zz * 8 + xx * 2 + cc, (s + dy) % 4)

    plane = [(dz, dx) for dz in range(4) for dx in range(4) if (dz, dx) != (0, 0)]
    plane.sort(key=lambda d: -min(d[0], 4 - d[0]) - min(d[1], 4 - d[1]))
    right, left, partner = dev(0, 0, 1, 0), dev(0, 0, 3, 0), dev(0, 0, 0, 1)

    barrier = pltpu.get_barrier_semaphore()
    friends = [dev(dz, dx, 0, 0) for dz, dx in plane]
    friends += [dev(0, 0, dy, dc) for dy in range(4) for dc in range(2) if (dy, dc) != (0, 0)]
    for f in friends:
        pl.semaphore_signal(barrier, inc=1, device_id=f, device_id_type=MESH)

    start_copy = pltpu.make_async_copy(start_hbm, start_ref, start_sem)
    start_copy.start()
    pieces = load_sem.shape[0]
    step = nb // pieces
    loads = []
    for i in range(pieces):
        rows = pl.ds(i * step, step)
        a = pltpu.make_async_copy(tin_hbm.at[rows], tin.at[rows], load_sem.at[i, 0])
        b = pltpu.make_async_copy(tout_hbm.at[rows], tout.at[rows], load_sem.at[i, 1])
        a.start()
        b.start()
        loads.append((a, b))

    own = s * nb
    table_copies = [
        pltpu.make_async_copy(a, b, table_sem.at[i])
        for i, (a, b) in enumerate(((ic_hbm, ic), (oc_hbm, oc), (exp_hbm, exp_ref), (recv_hbm, recv_ref)))
    ]
    for cp in table_copies:
        cp.start()

    def slot_of(i, carry):
        b, t = i // tp_out, i % tp_out
        v = oc[t, b]
        g, e = v // offered, v % offered
        oidx[t, b] = (g % 2) * (16 * offered) + (g // 2) * offered + recv_ref[e, g]
        return carry

    def total(ref, b, n):
        return mul(jnp.ones((16, n * tile), BF16), jnp.abs(ref[b].reshape(n * tile, tile)))

    def degrees(first, last):
        for i in range(first, last):
            for cp in loads[i]:
                cp.wait()

            def degree(b, carry):
                mag = (total(tin, b, tp_in) + total(tout, b, tp_out))[:1]
                inv = 1.0 / jnp.sqrt(mag / count + 1e-06)
                dall[pl.ds(own + b, 1), :] = inv
                dinv[b] = jnp.broadcast_to(inv, (8, tile))
                rowf[b] = jnp.broadcast_to(spectral * inv, (8, tile))
                return carry

            lax.fori_loop(i * step, (i + 1) * step, degree, 0, unroll=True)

    def degree_copies():
        block = dall.at[pl.ds(own, nb)]
        return [
            pltpu.make_async_remote_copy(
                src_ref=block, dst_ref=block, send_sem=d_send, recv_sem=d_recv,
                device_id=dev(0, 0, d, 0), device_id_type=MESH,
            )
            for d in (1, 2, 3)
        ]

    def degrees_end():
        view = dall.at[pl.ds(0, 3 * nb)]
        pltpu.make_async_copy(view, view, d_recv).wait()
        pltpu.make_async_copy(view, view, d_send).wait()

    base = core * (16 * offered) + (z * 4 + x) * offered

    def y_copies(j):
        part = raws[j] if j < NC else parts[(j // NC) % 2][j % NC]

        def cp(k, first, to):
            block = part.at[pl.ds(first, half)]
            return pltpu.make_async_remote_copy(
                src_ref=block, dst_ref=block, send_sem=y_send.at[j, k],
                recv_sem=y_recv.at[j, k], device_id=to, device_id_type=MESH,
            )

        lo = ((s + 3) % 4) * nb
        hi = ((s + 1) % 4) * nb
        sends = [cp(0, own, right), cp(1, own + half, left), cp(2, own + half, right), cp(3, own, left)]
        forwards = [cp(4, lo, right), cp(5, hi + half, left)]
        return sends, forwards

    def send_own(j, which=(0, 1, 2, 3)):
        sends = y_copies(j)[0]
        for k in which:
            sends[k].start()

    def forward(j):
        sends, forwards = y_copies(j)
        for k in range(2):
            sends[k].wait_recv()
            forwards[k].start()

    def xz_copies(j):
        out = outs[(j // NC) % 2][j % NC]
        block = out.at[pl.ds(base, offered)]
        return [
            pltpu.make_async_remote_copy(
                src_ref=block, dst_ref=block, send_sem=xz_send.at[j], recv_sem=xz_recv.at[j, (4 - dz) % 4],
                device_id=dev(dz, dx, 0, 0), device_id_type=MESH,
            )
            for dz, dx in plane
        ]

    def wait_bytes(out, sem, n):
        view = out.at[pl.ds(0, n * offered)]
        pltpu.make_async_copy(view, view, sem).wait()

    def export(j):
        sends, forwards = y_copies(j)
        sends[2].wait_recv()
        sends[3].wait_recv()
        for cp in forwards:
            cp.wait_recv()
        for cp in sends:
            cp.wait_send()
        part = parts[(j // NC) % 2][j % NC]
        out = outs[(j // NC) % 2][j % NC]
        if j < NC:

            def one(k, carry):
                part[k] = (raws[j][k].astype(F32) * dall[pl.ds(k, 1), :]).astype(BF16)
                return carry

            lax.fori_loop(0, 4 * nb, one, 0, unroll=8)
        for e in range(offered):
            out[base + e] = part[exp_ref[e]]
        for cp in xz_copies(j):
            cp.start()

    def core_copy(j, dz):
        row = core * (16 * offered) + ((z + dz) % 4) * (4 * offered)
        block = outs[(j // NC) % 2][j % NC].at[pl.ds(row, 4 * offered)]
        return pltpu.make_async_remote_copy(
            src_ref=block, dst_ref=block, send_sem=core_send.at[j, dz], recv_sem=core_recv.at[j, dz],
            device_id=partner, device_id_type=MESH,
        )

    def share(j):
        out = outs[(j // NC) % 2][j % NC]
        for dz in (0, 1, 3, 2):
            wait_bytes(out, xz_recv.at[j, dz], 3 if dz == 0 else 4)
            core_copy(j, dz).start()
        wait_bytes(out, xz_send.at[j], len(plane))
        for cp in y_copies(j)[1]:
            cp.wait_send()

    def inner(j, first, last):
        part, c = parts[(j // NC) % 2][j % NC], j % NC

        def one(b, carry):
            v = jnp.concatenate([part[ic[t, b]] for t in range(tp_in)], axis=1)
            acc[c, b] = jnp.dot(v, tin[b].reshape(tp_in * tile, tile), preferred_element_type=F32)
            return carry

        lax.fori_loop(first, last, one, 0, unroll=16)

    def scale(part, c, b, new):
        part[own + b] = (new * dinv[b, :1, :]).astype(BF16)

    def shared(j):
        for dz in range(4):
            core_copy(j, dz).wait_recv()
            core_copy(j, dz).wait_send()

    def outer(j, first, last):
        n, c = j // NC, j % NC
        out = outs[n % 2][c]
        rows = pl.ds(c * kc, kc)
        p = (n + 1) % 2

        def one(b, carry):
            v = jnp.concatenate([out[oidx[t, b]] for t in range(tp_out)], axis=1)
            o = acc[c, b] + jnp.dot(v, tout[b].reshape(tp_out * tile, tile), preferred_element_type=F32)
            new = o * rowf[b, :1, :]
            columns = pl.ds(pl.multiple_of(b * tile, tile), tile)
            if n == 0:
                vec[b, rows, :] = new
            elif n == 1:
                new = 2.0 * new - start_ref[rows, columns].astype(F32)
            elif n == 2:
                new = 2.0 * new - vec[b, rows, :]
                fil_high[rows, columns], fil_low[rows, columns] = split(new)
            else:
                image[:kc, columns], image[kc:, columns] = split(new)
            if n + 1 < OPS:
                scale(parts[p][c], c, b, new)
            return carry

        lax.fori_loop(first, last, one, 0, unroll=16)

    def product():
        high = fil_high[...]
        both = mul_nt(high, jnp.concatenate([high, fil_low[...]], axis=0))
        return both[:, :width] + both[:, width:] + mul_nt(fil_low[...], high)

    def rayleigh(j):
        both = mul_nt(image[...], fil_high[...])
        got = both[:kc] + both[kc:] + mul_nt(image[:kc, :], fil_low[...])
        ray[pl.ds((j % NC) * kc, kc), :] = got

    def spread(use, k):
        buf = (near, far)[k].at[use]
        if k == 0:
            block = buf.at[core * 4 + s]
            peers = [dev(0, 0, dy, dc) for dy in range(4) for dc in range(2) if (dy, dc) != (0, 0)]
        else:
            block = buf.at[z * 4 + x]
            peers = [dev(dz, dx, 0, 0) for dz, dx in plane]
        return [
            pltpu.make_async_remote_copy(
                src_ref=block, dst_ref=block, send_sem=sum_send.at[use, k], recv_sem=sum_recv.at[use, k],
                device_id=to, device_id_type=MESH,
            )
            for to in peers
        ]

    def sum_start(use, k, value):
        if k == 0:
            near[use, core * 4 + s] = value
        else:
            far[use, z * 4 + x] = value
        for cp in spread(use, k):
            cp.start()

    def sum_end(use, k):
        n = (8, 16)[k]
        buf = (near, far)[k].at[use]
        view = buf.at[pl.ds(0, n - 1)]
        pltpu.make_async_copy(view, view, sum_recv.at[use, k]).wait()
        pltpu.make_async_copy(view, view, sum_send.at[use, k]).wait()
        values = [buf[i] for i in range(n)]
        while len(values) > 1:
            values = [a + b for a, b in zip(values[::2], values[1::2])]
        return values[0]

    low = width // 2

    def pack(square):
        return jnp.concatenate([square[:low], square[low:]], axis=1)

    def unpack(packed):
        return jnp.concatenate([packed[:, :width], packed[:, width:]], axis=0)

    lane = lax.broadcasted_iota(jnp.int32, (1, 2 * width), 1)
    line = lax.broadcasted_iota(jnp.int32, (width, 1), 0)

    def eliminate(first, last):
        def one(k, carry):
            m = mat[...]
            row = mat[pl.ds(k, 1), :]
            inv = 1.0 / jnp.sqrt(jnp.sum(jnp.where(lane == k, row, 0.0), axis=1, keepdims=True))
            row = row * inv
            col = jnp.sum(jnp.where(lane == k, m, 0.0), axis=1, keepdims=True) * inv
            mat[...] = jnp.where(line > k, m - col * row, jnp.where(line == k, row, m))
            return carry

        lax.fori_loop(first, last, one, 0)

    def start_elimination(gram):
        eye = jnp.where(lane - width == line, 1.0, 0.0)
        gram = unpack(gram) / rows_total
        mat[...] = jnp.where(lane < width, jnp.concatenate([gram, gram], axis=1), eye)

    stages = OPS * NC

    def has(j):
        return 0 <= j < stages

    start_copy.wait()
    for b in range(nb):
        for c in range(NC):
            raws[c][own + b] = start_ref[c * kc : (c + 1) * kc, b * tile : (b + 1) * tile]
    pl.semaphore_wait(barrier, len(friends))
    send_own(0)
    for cp in table_copies:
        cp.wait()
    degrees(0, 3)
    send_own(1, (0, 1))
    forward(0)
    send_own(1, (2, 3))
    degrees(3, 6)
    send_own(2, (0, 1))
    forward(1)
    send_own(2, (2, 3))
    degrees(6, pieces)
    for cp in degree_copies():
        cp.start()
    send_own(3, (0, 1))
    forward(2)
    send_own(3, (2, 3))
    lax.fori_loop(0, nb * tp_out, slot_of, 0, unroll=8)
    degrees_end()
    export(0)
    for i in range(2, stages + NC):
        if has(i - 4):
            shared(i - 4)
            outer(i - 4, 0, half)
        if i >= NC and has(i - 1):
            forward(i - 1)
        if i >= NC and has(i):
            send_own(i, (0,))
        if has(i - 4):
            outer(i - 4, half, nb)
        if i >= NC and has(i):
            send_own(i, (1, 2, 3))
        if i - 4 >= stages - NC:
            rayleigh(i - 4)
        if i == 3:
            inner(1, 0, half)
        if has(i - 3):
            share(i - 3)
        if i == stages - 1:
            sum_start(0, 0, pack(product()))
        if i == stages:
            sum_start(0, 1, sum_end(0, 0))
        if has(i - 2):
            inner(i - 2, half if i == 3 else 0, nb)
        if has(i - 1):
            export(i - 1)

    sum_start(1, 0, pack(ray[...]))
    start_elimination(sum_end(0, 1))
    eliminate(0, 40)
    sum_start(1, 1, sum_end(1, 0))
    eliminate(40, width)
    linv = mat[...][:, width:]
    linv_high, linv_low = split(linv)
    linv_both = jnp.concatenate([linv_high, linv_low], axis=0)
    columns = 4 * tile

    def basis(first, last):
        for i in range(first, last):
            view = pl.ds(i * columns, columns)
            both = mul(linv_both, fil_high[:, view])
            basis_vmem[:, view] = both[:width] + both[width:] + mul(linv_high, fil_low[:, view])
            basis_copy(i).start()

    def basis_copy(i):
        view = pl.ds(i * columns, columns)
        return pltpu.make_async_copy(basis_vmem.at[:, view], basis_ref.at[:, view], basis_sem.at[i])

    groups = nb // 4
    basis(0, groups)
    rayleigh_t = unpack(sum_end(1, 1)) / rows_total
    proj_ref[...] = nt(nt(linv, rayleigh_t), linv)
    for i in range(groups):
        basis_copy(i).wait()


def deliver(basis, proj, basis_out, proj_out, held, held_proj, sem):
    width = basis.shape[1] // 4
    steps = []
    for i in range(5):
        if i < 4:
            part = (slice(None), pl.ds(i * width, width))
            refs = basis.at[part], held.at[part], basis_out.at[part]
        else:
            refs = proj, held_proj, proj_out
        steps.append(
            (pltpu.make_async_copy(refs[0], refs[1], sem.at[i, 0]),
             pltpu.make_async_copy(refs[1], refs[2], sem.at[i, 1]))
        )
    for come, _ in steps:
        come.start()
    for come, go in steps:
        come.wait()
        go.start()
    for _, go in steps:
        go.wait()


def body(start_block, tiles_in, tiles_out, in_cols, out_cols, export_list, recv_list):
    width, local_rows = start_block.shape
    nb, tp_in, tile, _ = tiles_in.shape
    tp_out = tiles_out.shape[1]
    count = (tp_in + tp_out) * tile
    devices = lax.axis_size("dom") * lax.axis_size("sub")
    kc = width // NC
    stages = OPS * NC
    blocks = nb * 4
    slots = recv_list.size
    hbm = pl.BlockSpec(memory_space=pl.ANY)
    vmem = pl.BlockSpec(memory_space=pltpu.VMEM)
    dma = pltpu.SemaphoreType.DMA
    outputs = pl.pallas_call(
        functools.partial(
            kernel, local_rows * devices, 1.0 / (1.25 * math.sqrt(count)), count
        ),
        out_shape=(
            jax.ShapeDtypeStruct((width, local_rows), F32),
            jax.ShapeDtypeStruct((width, width), F32),
        ),
        in_specs=[hbm] * 7,
        out_specs=(hbm, vmem),
        scratch_shapes=[
            pltpu.VMEM(start_block.shape, BF16),
            pltpu.VMEM(tiles_in.shape, BF16),
            pltpu.VMEM(tiles_out.shape, BF16),
            *[pltpu.VMEM((blocks, kc, tile), BF16) for _ in range(3 * NC)],
            *[pltpu.VMEM((slots, kc, tile), BF16) for _ in range(2 * NC)],
            pltpu.VMEM((nb, width, tile), F32),
            pltpu.VMEM((NC, nb, kc, tile), F32),
            pltpu.VMEM((nb, 8, tile), F32),
            pltpu.VMEM((nb, 8, tile), F32),
            pltpu.VMEM((blocks, tile), F32),
            pltpu.SMEM((tp_in, nb), jnp.int32),
            pltpu.SMEM((tp_out, nb), jnp.int32),
            pltpu.SMEM((export_list.size,), jnp.int32),
            pltpu.SMEM(recv_list.shape[:1:-1], jnp.int32),
            pltpu.SMEM((tp_out, nb), jnp.int32),
            pltpu.VMEM((width, local_rows), BF16),
            pltpu.VMEM((width, local_rows), BF16),
            pltpu.VMEM((2 * kc, local_rows), BF16),
            pltpu.VMEM((width, 2 * width), F32),
            pltpu.VMEM((width, width), F32),
            pltpu.VMEM((2, 8, width // 2, 2 * width), F32),
            pltpu.VMEM((2, 16, width // 2, 2 * width), F32),
            pltpu.VMEM((width, local_rows), F32),
            dma((4,)),
            dma,
            dma((8, 2)),
            dma,
            dma,
            dma((stages, 6)),
            dma((stages, 6)),
            dma((stages,)),
            dma((stages, 4)),
            dma((stages, 4)),
            dma((stages, 4)),
            dma((2, 2)),
            dma((2, 2)),
            dma((8,)),
        ],
        compiler_params=pltpu.CompilerParams(
            collective_id=0, has_side_effects=True, vmem_limit_bytes=60 << 20
        ),
        name="filtered_step",
    )(
        start_block, tiles_in, tiles_out, in_cols.T, out_cols.T,
        export_list.reshape(-1), recv_list[0, 0].T,
    )
    return pl.pallas_call(
        deliver,
        out_shape=tuple(jax.ShapeDtypeStruct(o.shape, o.dtype) for o in outputs),
        in_specs=[hbm, hbm],
        out_specs=(hbm, hbm),
        scratch_shapes=[*[pltpu.VMEM(o.shape, o.dtype) for o in outputs], dma((5, 2))],
        compiler_params=pltpu.CompilerParams(vmem_limit_bytes=60 << 20),
        name="deliver",
    )(*outputs)


def solution(mesh):
    return jax.shard_map(
        body,
        mesh=mesh,
        in_specs=(
            P(None, ("dom", "sub")),
            P(("dom", "sub"), None, None, None),
            P(("dom", "sub"), None, None, None),
            P(("dom", "sub"), None),
            P(("dom", "sub"), None),
            P("dom", "sub", None),
            P("dom", "sub", None, None),
        ),
        out_specs=(P(None, ("dom", "sub")), P()),
        check_vma=False,
    )
```
